32 devices in a mesh: parts: 2 (over x), expert: 4 (over z), hidden: 4 (over y, core).
Axes of the slice: x: 2, y: 2, z: 4, core: 2. Of those that a mesh axis runs over, the one named last changes fastest.
Arguments:
- tokens: bfloat16 [512, 3072], P(('parts', 'expert', 'hidden')), parts along dimension 0, may hold values from -6 to 6
- grad_out: bfloat16 [512, 3072], P(('parts', 'expert', 'hidden')), parts along dimension 0, may hold values from -6 to 6
- routes: int32 [512, 2], P(('parts', 'expert', 'hidden')), parts along dimension 0, may hold values from 0 to 3, all different within a row; in each aligned block of 16 rows (0 to 15, 16 to 31, ...) at most 12 rows name the same one
- w_router: bfloat16 [3072, 4], replicated, may hold values from -0.109375 to 0.109375
- w_gate: bfloat16 [4, 3072, 8192], P('expert', None, 'hidden'), may hold values from -0.109375 to 0.109375
- w_up: bfloat16 [4, 3072, 8192], P('expert', None, 'hidden'), may hold values from -0.109375 to 0.109375
- w_down: bfloat16 [4, 8192, 3072], P('expert', 'hidden'), may hold values from -0.0625 to 0.0625
Outputs:
- input_grad: bfloat16 [512, 3072], P(('parts', 'expert', 'hidden')), parts along dimension 0
- logit_grad: float32 [512, 2], P(('parts', 'expert', 'hidden')), parts along dimension 0
The draws below stay inside these ranges and needn't reach their ends.
There are 2 independent parts, one for each index of `parts`. The reference program is written for one: setup_inputs(seed, part) draws one part's arguments, and reference() takes and returns one part's arrays. A program takes and returns all parts, laid end to end along the dimension named above; an argument that names none is the same for every part. Nothing has to cross between parts.
Inputs may be any that keep to these rules, and one draw needn't show every extreme that they name: `routes`: the 2 experts of a row differ; the rows of one device name each expert at most 12 times, a bound that some block reaches.
All inputs are finite; a program needn't handle non-finite values.
Results may differ from the reference program's by a relative error of at most 0.005.
Values may be sent and summed in bfloat16 or wider, within the bound.
No kernel may reach another device: no remote copies, remote signals or barrier semaphores. Data moves between devices by JAX's collectives and lax.ppermute only.
A program may use at most 128 MiB of HBM per device.

```python
import math
import jax
import jax.numpy as jnp
import numpy as np
from jax import lax

D = 3072
FF = 8192
TOP = 2
TOK_DEV = 16
EXPERTS = 4
CAP = 12
TOKENS = 256
N_EXPERT = 4
N_HIDDEN = 4


def block_scale(rng, extent, cuts, least, largest):
    def one(dim, blocks):
        draws = jax.random.uniform(jax.random.fold_in(jax.random.fold_in(rng, 6), dim), (blocks,), jnp.float32, least / len(cuts), largest / len(cuts))
        return jnp.repeat(jnp.exp(draws), extent[dim] // blocks).reshape((-1,) + (1,) * (len(extent) - dim - 1))

    loudness = one(*cuts[0])
    for cut in cuts[1:]:
        loudness = loudness * one(*cut)
    return loudness


def routed_block(own_key, own, number, rows, amount, top, bound, lean):
    sequence = jax.random.permutation(own_key, amount)
    crowded, ordinary = load_shares(amount, rows * top, bound, lean, True), load_shares(amount, rows * top, bound, lean, False)
    places = jnp.arange(amount)

    def named(tallies, rotation):
        used = int((tallies > 0).sum())
        fixed = max(1, used // 4)
        shifted = fixed + (places - fixed + rotation * (used - fixed)) % max(1, amount - fixed)
        return jnp.zeros((amount,), jnp.int32).at[sequence[jnp.where(places < fixed, places, shifted)]].set(jnp.asarray(tallies, jnp.int32))

    tallies = jnp.where(number % 4 == 0, named(crowded, number // 4), named(ordinary, number - number // 4 - 1))
    mixed = jax.random.permutation(jax.random.fold_in(own, 3), amount)
    source_of, taker = mixed[0:amount // 2 * 2:2], mixed[1:amount // 2 * 2:2]
    slack = jnp.minimum(tallies[source_of] - 1, bound - tallies[taker]) // 2
    slack = jnp.where((source_of == sequence[0]) | (taker == sequence[0]) | (tallies[taker] == 0), 0, jnp.maximum(slack, 0))
    shifted = jax.random.randint(jax.random.fold_in(own, 4), (amount // 2,), 0, 1 << 20) % (slack + 1)
    tallies = tallies.at[source_of].add(-shifted).at[taker].add(shifted)
    items = jnp.searchsorted(jnp.cumsum(tallies), jnp.arange(rows * top), side="right").astype(jnp.int32)
    listing = items.reshape(top, rows).T
    listing = listing[jax.random.permutation(jax.random.fold_in(own, 1), rows)]
    rotation = jax.random.randint(jax.random.fold_in(own, 2), (rows, 1), 0, top)
    return jnp.take_along_axis(listing, (jnp.arange(top)[None, :] + rotation) % top, axis=1)


def load_shares(amount, total, bound, lean, full):
    weights = [(1 << 20) // math.isqrt(grade ** lean) + 1 for grade in range(1, amount + 1)]
    largest = bound if full else min(bound, max(-(-total // amount), total * weights[0] // sum(weights)))
    least = 1 if total - largest >= amount - 1 else 0
    holding, rest = [largest] + [least] * (amount - 1), total - largest - least * (amount - 1)
    while rest > 0:
        movable = [i for i in range(1, amount) if holding[i] < largest] or [i for i in range(1, amount) if holding[i] < bound]
        whole, left = sum([weights[i] for i in movable]), rest
        for i in movable:
            more = min(bound - holding[i], max(1, left * weights[i] // whole), rest)
            holding[i] = holding[i] + more
            rest = rest - more
    return np.array(holding)


def noise(key, shape, scale, limit, split=(), kind=jnp.bfloat16):
    drawn = jax.random.normal(key, shape, jnp.float32) * scale
    if len(split) > 0:
        drawn = block_scale(key, shape, split, -0.22, 0.18) * drawn
    return jnp.clip(drawn, min=-limit, max=limit).astype(kind)


def setup_inputs(seed: int = 0, part: int = 0) -> dict:
    streams_of = jax.random.split(jax.random.key(seed), 8)
    part_keys = jax.random.split(jax.random.fold_in(streams_of[7], part), 8)
    tokens = noise(part_keys[0], (TOKENS, D), 1.0, 6.0, ((0, 16),))
    grad_out = noise(part_keys[1], (TOKENS, D), 1.0, 6.0, ((0, 16),))
    routes_keys = jax.random.split(jax.random.fold_in(part_keys[2], 1), TOKENS // TOK_DEV)
    routes_turns = jax.random.permutation(jax.random.fold_in(part_keys[2], 3), TOKENS // TOK_DEV)
    routes = jax.vmap(lambda own, number: routed_block(jax.random.fold_in(part_keys[2], 2), own, number, TOK_DEV, EXPERTS, TOP, CAP, 2))(routes_keys, routes_turns).reshape((TOKENS, TOP))
    w_router = noise(streams_of[3], (D, EXPERTS), D ** -0.5, 0.109375)
    w_gate = noise(streams_of[4], (EXPERTS, D, FF), D ** -0.5, 0.109375, ((0, 4), (2, 4)))
    w_up = noise(streams_of[5], (EXPERTS, D, FF), D ** -0.5, 0.109375, ((0, 4), (2, 4)))
    w_down = noise(streams_of[6], (EXPERTS, FF, D), FF ** -0.5, 0.0625, ((0, 4), (1, 4)))
    return {"tokens": tokens, "grad_out": grad_out, "routes": routes, "w_router": w_router, "w_gate": w_gate, "w_up": w_up, "w_down": w_down}


def reference(tokens, grad_out, routes, w_router, w_gate, w_up, w_down):
    logits = jnp.dot(tokens, w_router, preferred_element_type=jnp.float32)
    chosen = jnp.take_along_axis(logits, routes, axis=1)
    prob = jax.nn.sigmoid(chosen - chosen[:, ::-1])
    flat = routes.reshape(-1)
    token_of = (jnp.arange(flat.shape[0], dtype=jnp.int32) // TOP).astype(jnp.int32)
    row_count = N_EXPERT * N_HIDDEN * CAP

    def per_expert(expert_id):
        order = jnp.argsort((flat != expert_id).astype(jnp.int32), stable=True)[:row_count].astype(jnp.int32)
        live = flat[order] == expert_id
        picked = token_of[order]
        x_rows = tokens[picked]
        dy_rows = grad_out[picked]
        gate = jnp.dot(x_rows, w_gate[expert_id], preferred_element_type=jnp.float32)
        up = jnp.dot(x_rows, w_up[expert_id], preferred_element_type=jnp.float32)
        back = jnp.dot(dy_rows, w_down[expert_id].T, preferred_element_type=jnp.float32)
        sig = jax.nn.sigmoid(gate)
        silu = gate * sig
        score = jnp.sum(silu * up * back, axis=1)
        d_gate = (back * up * sig * (1.0 + gate * (1.0 - sig))).astype(jnp.bfloat16)
        d_up = (back * silu).astype(jnp.bfloat16)
        rows_back = jnp.dot(d_gate, w_gate[expert_id].T, preferred_element_type=jnp.float32)
        rows_back = rows_back + jnp.dot(d_up, w_up[expert_id].T, preferred_element_type=jnp.float32)
        rows_back = jnp.where(live[:, None], rows_back, jnp.float32(0.0))
        score = jnp.where(live, score, jnp.float32(0.0))
        return order, rows_back, score

    orders, backs, scores = lax.map(per_expert, jnp.arange(N_EXPERT, dtype=jnp.int32))
    orders = orders.reshape(-1)
    route_back = jnp.zeros((flat.shape[0], tokens.shape[1]), jnp.float32).at[orders].add(backs.reshape(-1, tokens.shape[1]))
    route_score = jnp.zeros((flat.shape[0],), jnp.float32).at[orders].add(scores.reshape(-1))
    route_back = route_back.reshape(tokens.shape[0], TOP, tokens.shape[1])
    route_score = route_score.reshape(tokens.shape[0], TOP)
    logit_grad = prob[:, 0:1] * prob[:, 1:2] * (route_score - route_score[:, ::-1])
    labels = jnp.arange(N_EXPERT, dtype=jnp.int32)
    onehot = (routes[:, :, None] == labels).astype(jnp.float32)
    spread = jnp.einsum('tk,tke->te', logit_grad, onehot)
    router_term = jnp.dot(spread, w_router.astype(jnp.float32).T, precision=lax.Precision.HIGHEST)
    input_grad = (jnp.sum(prob[:, :, None] * route_back, axis=1) + router_term).astype(jnp.bfloat16)
    return input_grad, logit_grad
```

```python
import functools

import jax
import jax.numpy as jnp
from jax import lax
from jax.experimental import pallas as pl
from jax.experimental.pallas import tpu as pltpu
from jax.sharding import PartitionSpec as P

BF = jnp.bfloat16
F32 = jnp.float32
LANES = 128
ROWS = 256
AHEAD = 3
NT = (((1,), (1,)), ((), ()))
ANY = pl.BlockSpec(memory_space=pl.ANY)
VMEM = pl.BlockSpec(memory_space=pltpu.VMEM)


def dot_nt(a, b):
    return lax.dot_general(a, b, NT, preferred_element_type=F32)


def chunk(extent, wanted):
    size = min(extent, wanted)
    while extent % size:
        size -= LANES
    return size


def fetch(pieces, held, sems):
    copies, at = [], 0
    for i, piece in enumerate(pieces):
        rows = piece.shape[0]
        copies.append(pltpu.make_async_copy(piece, held.at[pl.ds(at, rows)], sems.at[i]))
        at += rows
    for copy in copies:
        copy.start()
    for copy in copies:
        copy.wait()


def load_kernel(n, *refs):
    sources, target, sems = refs[:n], refs[n], refs[n + 1]
    copies = [pltpu.make_async_copy(a, target.at[i], sems.at[i]) for i, a in enumerate(sources)]
    for copy in copies:
        copy.start()
    for copy in copies:
        copy.wait()


def gate_up_kernel(n, *refs):
    pieces, (w_both, both, held, sems) = refs[:n], refs[n:]
    w_gate, w_up, gate, up = w_both.at[0], w_both.at[1], both.at[0], both.at[1]
    fetch(pieces, held, sems)
    rows, ff = gate.shape
    block, step = min(rows, ROWS), chunk(ff, 512)

    @pl.loop(0, rows // block)
    def _(r):
        at = pl.ds(pl.multiple_of(r * block, block), block)

        @pl.loop(0, ff // step)
        def _(f):
            cols = pl.ds(pl.multiple_of(f * step, step), step)
            gate[at, cols] = jnp.dot(held[at, :], w_gate[:, cols], preferred_element_type=F32)
            up[at, cols] = jnp.dot(held[at, :], w_up[:, cols], preferred_element_type=F32)


def split3(score):
    high = score.astype(BF)
    rest = score - high.astype(F32)
    mid = rest.astype(BF)
    low = (rest - mid.astype(F32)).astype(BF)
    lane = lax.broadcasted_iota(jnp.int32, (score.shape[0], LANES), 1)
    spread = [jnp.broadcast_to(t.astype(F32), lane.shape) for t in (high, mid, low)]
    out = jnp.where(lane == 0, spread[0], jnp.where(lane == 1, spread[1], spread[2]))
    return jnp.where(lane < 3, out, 0.0).astype(BF)


def join3(tail):
    return jnp.sum(tail.astype(F32), axis=1, keepdims=True)


def back_kernel(n, *refs):
    pieces = refs[:n]
    w_gate, w_up, w_down, both, keep, send = refs[n : n + 6]
    held, d_gate, d_up, score, v_gate, v_up, v_down, sems, down_sems, sum_sems = refs[n + 6 :]
    gate, up = both.at[0], both.at[1]
    rows, ff = gate.shape
    width = held.shape[1]
    block, step, dstep = min(rows, ROWS), chunk(ff, 512), chunk(width, 512)
    half = rows // 2

    def load_down(f):
        part = pl.ds(pl.multiple_of(f * step, step), step)
        return pltpu.make_async_copy(w_down.at[part], v_down.at[part], down_sems.at[f])

    def load_sum(d, k):
        part = pl.ds(pl.multiple_of(d * dstep, dstep), dstep)
        source, target = ((w_gate, v_gate), (w_up, v_up))[k]
        return pltpu.make_async_copy(source.at[part], target.at[part], sum_sems.at[k, d])

    downs, sums = ff // step, width // dstep

    def start(i):
        @pl.when(i < downs)
        def _():
            load_down(i).start()

        @pl.when((i >= downs) & (i < downs + sums))
        def _():
            load_sum(i - downs, 0).start()
            load_sum(i - downs, 1).start()

    load_down(0).start()
    fetches, at = [], 0
    for i, piece in enumerate(pieces):
        fetches.append(pltpu.make_async_copy(piece, held.at[pl.ds(at, piece.shape[0])], sems.at[i]))
        at += piece.shape[0]
    for copy in fetches:
        copy.start()
    for i in range(1, AHEAD):
        start(i)
    for copy in fetches:
        copy.wait()

    @pl.loop(0, rows // block)
    def _(r):
        at = pl.ds(pl.multiple_of(r * block, block), block)
        score[at, :] = jnp.zeros((block, 1), F32)

        @pl.loop(0, ff // step)
        def _(f):
            cols = pl.ds(pl.multiple_of(f * step, step), step)

            @pl.when(r == 0)
            def _():
                load_down(f).wait()
                start(f + AHEAD)

            back = dot_nt(held[at, :], v_down[cols, :])
            g, u = gate[at, cols], up[at, cols]
            sig = jax.nn.sigmoid(g)
            silu = g * sig
            score[at, :] += jnp.sum(silu * u * back, axis=1, keepdims=True)
            d_gate[at, cols] = (back * u * sig * (1.0 + g * (1.0 - sig))).astype(BF)
            d_up[at, cols] = (back * silu).astype(BF)

        @pl.loop(0, width // dstep)
        def _(d):
            cols = pl.ds(pl.multiple_of(d * dstep, dstep), dstep)

            @pl.when(r == 0)
            def _():
                load_sum(d, 0).wait()
                load_sum(d, 1).wait()
                start(d + downs + AHEAD)

            value = dot_nt(d_gate[at, :], v_gate[cols, :]) + dot_nt(d_up[at, :], v_up[cols, :])
            value = value.astype(BF)
            if rows == block:
                keep[:, cols] = value[:half]
                send[:, cols] = value[half:]
            else:

                @pl.when(r < half // block)
                def _():
                    keep[at, cols] = value

                @pl.when(r >= half // block)
                def _():
                    send[pl.ds(pl.multiple_of(r * block - half, block), block), cols] = value

    keep[:, pl.ds(width, LANES)] = split3(score[pl.ds(0, half), :])
    send[:, pl.ds(width, LANES)] = split3(score[pl.ds(half, half), :])


def add_kernel(mine, theirs, *outs):
    width = mine.shape[1] - LANES
    at = 0
    for out in outs:
        rows = out.shape[0]
        here = pl.ds(at, rows)
        total = mine[here, pl.ds(0, width)].astype(F32) + theirs[here, pl.ds(0, width)].astype(F32)
        out[:, pl.ds(0, width)] = total.astype(BF)
        tail = join3(mine[here, pl.ds(width, LANES)]) + join3(theirs[here, pl.ds(width, LANES)])
        out[:, pl.ds(width, LANES)] = split3(tail)
        at += rows


def route_kernel(tokens, w_router, routes, relative, weight, sign, pair):
    experts = w_router.shape[1]
    logits = jnp.dot(tokens[...], w_router[...], preferred_element_type=F32)
    label = lax.broadcasted_iota(jnp.int32, logits.shape, 1)
    first, second = label == routes[:, 0:1], label == routes[:, 1:2]
    chosen = [jnp.sum(jnp.where(m, logits, 0.0), axis=1, keepdims=True) for m in (first, second)]
    prob = [jax.nn.sigmoid(chosen[0] - chosen[1]), jax.nn.sigmoid(chosen[1] - chosen[0])]
    pair[...] = jnp.where(first, 1.0, 0.0) - jnp.where(second, 1.0, 0.0)
    first, second = label == relative[:, 0:1], label == relative[:, 1:2]
    weight[:, pl.ds(0, experts)] = jnp.where(first, prob[0], 0.0) + jnp.where(second, prob[1], 0.0)
    weight[:, pl.ds(experts, 1)] = prob[0] * prob[1]
    sign[...] = jnp.where(first, 1.0, 0.0) - jnp.where(second, 1.0, 0.0)


def final_kernel(n, *refs):
    blocks, (weight, sign, pair, router, out, logit_grad) = refs[:n], refs[n:]
    width = out.shape[1]
    total, gap = 0.0, 0.0
    for s, block in enumerate(blocks):
        total = total + weight[:, s : s + 1] * block[:, pl.ds(0, width)].astype(F32)
        gap = gap + sign[:, s : s + 1] * join3(block[:, pl.ds(width, LANES)])
    grad = weight[:, n : n + 1] * gap
    for e in range(n):
        total = total + (grad * pair[:, e : e + 1]) * router[e : e + 1, :]
    out[...] = total.astype(BF)
    logit_grad[:, 0:1] = grad
    logit_grad[:, 1:2] = -grad


def call(kernel, args, outs, specs, scratch=(), limit=None, cost=None):
    return pl.pallas_call(
        kernel,
        out_shape=outs,
        in_specs=specs,
        out_specs=[VMEM] * len(outs),
        scratch_shapes=list(scratch),
        compiler_params=pltpu.CompilerParams(vmem_limit_bytes=limit),
        cost_estimate=cost,
    )(*args)


def shards(hidden, tokens, grad_out, routes, w_router, w_gate, w_up, w_down):
    own, width = tokens.shape
    experts = w_router.shape[1]
    ff = w_gate.shape[2]
    shape = jax.ShapeDtypeStruct
    bits = []
    while (1 << len(bits)) < hidden:
        bits.append(1 << len(bits))
    bits = bits[1:] + bits[:1]

    def along(x, shift):
        return lax.ppermute(x, "expert", [(i, (i + shift) % experts) for i in range(experts)])

    def across(x, bit):
        return lax.ppermute(x, "hidden", [(i, i ^ bit) for i in range(hidden)])

    def near(x):
        pieces = [jnp.concatenate([x] + [along(x, s) for s in range(1, experts)])]
        for bit in bits[:-1]:
            pieces = pieces + [across(piece, bit) for piece in pieces]
        return pieces

    def far(pieces):
        return pieces + [across(piece, bits[-1]) for piece in pieces]

    rows = own * experts * hidden
    spare = (4 if rows <= ROWS else 12) << 20
    small = own * hidden * experts * (width + LANES) * 4 + (1 << 20)
    def load(*arrays):
        n = len(arrays)
        (loaded,) = call(
            functools.partial(load_kernel, n),
            arrays,
            [shape((n, *arrays[0].shape), BF)],
            [pl.BlockSpec(memory_space=pltpu.HBM)] * n,
            [pltpu.SemaphoreType.DMA((n,))],
            1 << 20,
            pl.CostEstimate(flops=0, bytes_accessed=2 * sum(a.size for a in arrays), transcendentals=0),
        )
        return pltpu.with_memory_space_constraint(loaded, pltpu.VMEM)

    sources = [pltpu.with_memory_space_constraint(w[0], pltpu.HBM) for w in (w_gate, w_up, w_down)]
    w_both = load(*sources[:2])
    x_pieces, dy_pieces = far(near(tokens)), near(grad_out)
    n = len(x_pieces)
    macs = rows * width * ff
    (both,) = call(
        functools.partial(gate_up_kernel, n),
        x_pieces + [w_both],
        [shape((2, rows, ff), F32)],
        [ANY] * n + [VMEM],
        [pltpu.VMEM((rows, width), BF), pltpu.SemaphoreType.DMA((n,))],
        rows * width * 2 + spare,
        pl.CostEstimate(flops=4 * macs, bytes_accessed=4 * width * ff, transcendentals=0),
    )
    *late, both = lax.optimization_barrier((*dy_pieces[1:], both))
    dy_pieces = [pltpu.with_memory_space_constraint(p, pltpu.HBM) for p in far(dy_pieces[:1] + late)]
    keep, send = call(
        functools.partial(back_kernel, n),
        dy_pieces + sources + [both],
        [shape((rows // 2, width + LANES), BF)] * 2,
        [ANY] * (n + 3) + [VMEM],
        [
            pltpu.VMEM((rows, width), BF),
            pltpu.VMEM((rows, ff), BF),
            pltpu.VMEM((rows, ff), BF),
            pltpu.VMEM((rows, 1), F32),
            pltpu.VMEM((width, ff), BF),
            pltpu.VMEM((width, ff), BF),
            pltpu.VMEM((ff, width), BF),
            pltpu.SemaphoreType.DMA((n,)),
            pltpu.SemaphoreType.DMA((ff // chunk(ff, 512),)),
            pltpu.SemaphoreType.DMA((2, width // chunk(width, 512))),
        ],
        6 * width * ff + rows * (width + LANES) * 4 + rows * (ff * 4 + 4 * LANES) + spare,
        pl.CostEstimate(flops=6 * macs, bytes_accessed=6 * width * ff, transcendentals=0),
    )
    relative = (routes - lax.axis_index("expert")) % experts
    weight, sign, pair = call(
        route_kernel,
        [tokens, w_router, routes, relative],
        [shape((own, experts + 1), F32), shape((own, experts), F32), shape((own, experts), F32)],
        [VMEM] * 4,
        limit=small,
    )
    for bit in bits[:0:-1]:
        arrived = across(send, bit)
        part = keep.shape[0] // 2
        keep, send = call(
            add_kernel, [keep, arrived], [shape((part, width + LANES), BF)] * 2, [VMEM] * 2, limit=small
        )
    arrived = across(send, bits[0])
    blocks = call(
        add_kernel, [keep, arrived], [shape((own, width + LANES), BF)] * experts, [VMEM] * 2, limit=small
    )
    blocks = [blocks[0]] + [along(blocks[s], experts - s) for s in range(1, experts)]
    input_grad, logit_grad = call(
        functools.partial(final_kernel, experts),
        blocks + [weight, sign, pair, w_router.astype(F32).T],
        [shape((own, width), BF), shape((own, 2), F32)],
        [VMEM] * (experts + 4),
        limit=small,
    )
    return (input_grad, logit_grad)


def solution(mesh):
    row = P(("parts", "expert", "hidden"), None)
    placed = (
        row,
        row,
        row,
        P(),
        P("expert", None, "hidden"),
        P("expert", None, "hidden"),
        P("expert", "hidden", None),
    )
    return jax.shard_map(
        functools.partial(shards, mesh.shape["hidden"]),
        mesh=mesh,
        in_specs=placed,
        out_specs=(row, row),
        check_vma=False,
    )
```

```python
import functools

import jax
import jax.numpy as jnp
from jax import lax
from jax.experimental import pallas as pl
from jax.experimental.pallas import tpu as pltpu
from jax.sharding import PartitionSpec as P

BF = jnp.bfloat16
F32 = jnp.float32
LANES = 128
ROWS = 256
GRANT = 19 << 20
AHEAD = 2
NT = (((1,), (1,)), ((), ()))
ANY = pl.BlockSpec(memory_space=pl.ANY)
VMEM = pl.BlockSpec(memory_space=pltpu.VMEM)


def dot_nt(a, b):
    return lax.dot_general(a, b, NT, preferred_element_type=F32)


def chunk(extent, wanted):
    size = min(extent, wanted)
    while extent % size:
        size -= LANES
    return size


def fetch(pieces, held, sems):
    copies, at = [], 0
    for i, piece in enumerate(pieces):
        rows = piece.shape[0]
        copies.append(pltpu.make_async_copy(piece, held.at[pl.ds(at, rows)], sems.at[i]))
        at += rows
    for copy in copies:
        copy.start()
    for copy in copies:
        copy.wait()


def load_kernel(first, second, target, sems):
    copies = [pltpu.make_async_copy(w, target.at[i], sems.at[i]) for i, w in enumerate((first, second))]
    for copy in copies:
        copy.start()
    for copy in copies:
        copy.wait()


def gate_up_kernel(n, *refs):
    pieces, (weights, both, _, held, sems) = refs[:n], refs[n:]
    fetch(pieces, held, sems)
    rows, ff = both.shape[1:]
    block, step = min(rows, ROWS), chunk(ff, 512)

    @pl.loop(0, rows // block)
    def _(r):
        at = pl.ds(pl.multiple_of(r * block, block), block)

        @pl.loop(0, ff // step)
        def _(f):
            cols = pl.ds(pl.multiple_of(f * step, step), step)
            for k in range(2):
                both[k, at, cols] = jnp.dot(held[at, :], weights[k, :, cols], preferred_element_type=F32)


def split3(score):
    high = score.astype(BF)
    rest = score - high.astype(F32)
    mid = rest.astype(BF)
    low = (rest - mid.astype(F32)).astype(BF)
    lane = lax.broadcasted_iota(jnp.int32, (score.shape[0], LANES), 1)
    spread = [jnp.broadcast_to(t.astype(F32), lane.shape) for t in (high, mid, low)]
    out = jnp.where(lane == 0, spread[0], jnp.where(lane == 1, spread[1], spread[2]))
    return jnp.where(lane < 3, out, 0.0).astype(BF)


def join3(tail):
    return jnp.sum(tail.astype(F32), axis=1, keepdims=True)


def store_halves(r, block, rows, cols, value, keep, send):
    half = rows // 2
    if rows == block:
        keep[:, cols] = value[:half]
        send[:, cols] = value[half:]
    else:

        @pl.when(r < half // block)
        def _():
            keep[pl.ds(pl.multiple_of(r * block, block), block), cols] = value

        @pl.when(r >= half // block)
        def _():
            send[pl.ds(pl.multiple_of(r * block - half, block), block), cols] = value


def sum_columns(start, width, r, block, grads, weights, keep, send):
    rows = grads.shape[1]
    at = pl.ds(pl.multiple_of(r * block, block), block)
    step = chunk(width, 512)

    @pl.loop(0, width // step)
    def _(d):
        source = pl.ds(pl.multiple_of(start + d * step, step), step)
        cols = pl.ds(pl.multiple_of(d * step, step), step)
        value = dot_nt(grads[0, at, :], weights[0, source, :])
        value = value + dot_nt(grads[1, at, :], weights[1, source, :])
        store_halves(r, block, rows, cols, value.astype(BF), keep, send)


def back_kernel(n, *refs):
    pieces = refs[:n]
    weights, w_down, both, keep, send, grads, score, _, held, v_down, sems, down_sems = refs[n:]
    rows, ff = both.shape[1:]
    block, step = min(rows, ROWS), chunk(ff, 512)

    def load_down(f):
        part = pl.ds(pl.multiple_of(f * step, step), step)
        return pltpu.make_async_copy(w_down.at[part], v_down.at[part], down_sems.at[f])

    load_down(0).start()
    fetch(pieces, held, sems)
    for f in range(1, min(AHEAD, ff // step)):
        load_down(f).start()

    @pl.loop(0, rows // block)
    def _(r):
        at = pl.ds(pl.multiple_of(r * block, block), block)
        score[at, :] = jnp.zeros((block, 1), F32)

        @pl.loop(0, ff // step)
        def _(f):
            cols = pl.ds(pl.multiple_of(f * step, step), step)

            @pl.when(r == 0)
            def _():
                load_down(f).wait()

                @pl.when(f + AHEAD < ff // step)
                def _():
                    load_down(f + AHEAD).start()

            back = dot_nt(held[at, :], v_down[cols, :])
            g, u = both[0, at, cols], both[1, at, cols]
            sig = jax.nn.sigmoid(g)
            silu = g * sig
            score[at, :] += jnp.sum(silu * u * back, axis=1, keepdims=True)
            grads[0, at, cols] = (back * u * sig * (1.0 + g * (1.0 - sig))).astype(BF)
            grads[1, at, cols] = (back * silu).astype(BF)

        sum_columns(0, keep.shape[1], r, block, grads, weights, keep, send)


def rest_kernel(start, weights, grads, score, keep, send):
    rows = grads.shape[1]
    width = keep.shape[1] - LANES
    block, half = min(rows, ROWS), rows // 2

    @pl.loop(0, rows // block)
    def _(r):
        sum_columns(start, width, r, block, grads, weights, keep, send)

    keep[:, pl.ds(width, LANES)] = split3(score[pl.ds(0, half), :])
    send[:, pl.ds(width, LANES)] = split3(score[pl.ds(half, half), :])


def add_kernel(tail, mine, theirs, *outs):
    width = mine.shape[1] - (LANES if tail else 0)
    at = 0
    for out in outs:
        rows = out.shape[0]
        here = pl.ds(at, rows)
        total = mine[here, pl.ds(0, width)].astype(F32) + theirs[here, pl.ds(0, width)].astype(F32)
        out[:, pl.ds(0, width)] = total.astype(BF)
        if tail:
            last = pl.ds(width, LANES)
            out[:, last] = split3(join3(mine[here, last]) + join3(theirs[here, last]))
        at += rows


def route_kernel(tokens, w_router, routes, relative, weight, sign, pair):
    experts = w_router.shape[1]
    logits = jnp.dot(tokens[...], w_router[...], preferred_element_type=F32)
    label = lax.broadcasted_iota(jnp.int32, logits.shape, 1)
    first, second = label == routes[:, 0:1], label == routes[:, 1:2]
    chosen = [jnp.sum(jnp.where(m, logits, 0.0), axis=1, keepdims=True) for m in (first, second)]
    prob = [jax.nn.sigmoid(chosen[0] - chosen[1]), jax.nn.sigmoid(chosen[1] - chosen[0])]
    pair[...] = jnp.where(first, 1.0, 0.0) - jnp.where(second, 1.0, 0.0)
    first, second = label == relative[:, 0:1], label == relative[:, 1:2]
    weight[:, pl.ds(0, experts)] = jnp.where(first, prob[0], 0.0) + jnp.where(second, prob[1], 0.0)
    weight[:, pl.ds(experts, 1)] = prob[0] * prob[1]
    sign[...] = jnp.where(first, 1.0, 0.0) - jnp.where(second, 1.0, 0.0)


def final_kernel(n, *refs):
    first, second, (weight, sign, pair, router, out, logit_grad) = refs[:n], refs[n : 2 * n], refs[2 * n :]
    lead = first[0].shape[1]
    gap = 0.0
    for s, block in enumerate(second):
        gap = gap + sign[:, s : s + 1] * join3(block[:, pl.ds(out.shape[1] - lead, LANES)])
    grad = weight[:, n : n + 1] * gap
    logit_grad[:, 0:1] = grad
    logit_grad[:, 1:2] = -grad
    for blocks, cols in ((first, pl.ds(0, lead)), (second, pl.ds(lead, out.shape[1] - lead))):
        total = 0.0
        for s, block in enumerate(blocks):
            total = total + weight[:, s : s + 1] * block[:, pl.ds(0, cols.size)].astype(F32)
        for e in range(n):
            total = total + (grad * pair[:, e : e + 1]) * router[e : e + 1, cols]
        out[:, cols] = total.astype(BF)


def call(kernel, args, outs, specs, scratch=(), limit=None, cost=None, alias={}):
    return pl.pallas_call(
        kernel,
        out_shape=outs,
        in_specs=specs,
        out_specs=[VMEM] * len(outs),
        scratch_shapes=list(scratch),
        compiler_params=pltpu.CompilerParams(vmem_limit_bytes=limit),
        cost_estimate=cost,
        input_output_aliases=alias,
    )(*args)


def shards(hidden, tokens, grad_out, routes, w_router, w_gate, w_up, w_down):
    own, width = tokens.shape
    experts = w_router.shape[1]
    ff = w_gate.shape[2]
    shape = jax.ShapeDtypeStruct
    bits = []
    while (1 << len(bits)) < hidden:
        bits.append(1 << len(bits))
    bits = bits[1:] + bits[:1]

    def along(x, shift):
        return lax.ppermute(x, "expert", [(i, (i + shift) % experts) for i in range(experts)])

    def across(x, bit):
        return lax.ppermute(x, "hidden", [(i, i ^ bit) for i in range(hidden)])

    rows = own * experts * hidden
    macs = rows * width * ff
    lead = width // 2
    rest = width - lead + LANES
    resident_bytes = rows * (2 * width + 8 * LANES) + rows * (ff * 4 + lead * 2 + rest * 2)
    grant = GRANT if rows <= ROWS else resident_bytes + GRANT
    small = min(rows, 2048) * (width + LANES) * 4 + (1 << 20)

    def cost(weights, matmuls):
        return pl.CostEstimate(
            flops=int(2 * matmuls * macs), bytes_accessed=2 * weights * width * ff, transcendentals=0
        )

    def vmem(x):
        return pltpu.with_memory_space_constraint(x, pltpu.VMEM)

    def hbm(x):
        return pltpu.with_memory_space_constraint(x, pltpu.HBM)

    def column(x):
        return jnp.concatenate([x] + [along(x, s) for s in range(1, experts)])

    def spread(pieces, some):
        for bit in some:
            pieces = pieces + [across(piece, bit) for piece in pieces]
        return pieces

    w_gate, w_up, w_down = [hbm(w[0]) for w in (w_gate, w_up, w_down)]
    held = pltpu.VMEM((rows, width), BF)
    pair_of = shape((2, *w_gate.shape), BF)
    (weights,) = call(
        load_kernel, [w_gate, w_up], [pair_of], [ANY] * 2, [pltpu.SemaphoreType.DMA((2,))], grant, cost(2, 0)
    )
    x_column, weights = lax.optimization_barrier((column(tokens), vmem(weights)))
    x_column, grad_out = lax.optimization_barrier((x_column, grad_out))
    x_pieces = spread([x_column], bits)
    dy_pieces = spread([column(grad_out)], bits[:-1])
    n = len(x_pieces)
    both, weights = call(
        functools.partial(gate_up_kernel, n),
        x_pieces + [weights],
        [shape((2, rows, ff), F32), pair_of],
        [ANY] * n + [VMEM],
        [held, pltpu.SemaphoreType.DMA((n,))],
        grant,
        cost(2, 2),
        {n: 1},
    )
    both, weights = vmem(both), vmem(weights)
    *late, both = lax.optimization_barrier((*dy_pieces[1:], both))
    dy_pieces = spread(dy_pieces[:1] + late, bits[-1:])
    keep, send, grads, score, weights = call(
        functools.partial(back_kernel, n),
        dy_pieces + [weights, w_down, both],
        [shape((rows // 2, lead), BF)] * 2 + [shape((2, rows, ff), BF), shape((rows, 1), F32), pair_of],
        [ANY] * n + [VMEM, ANY, VMEM],
        [
            held,
            pltpu.VMEM((ff, width), BF),
            pltpu.SemaphoreType.DMA((n,)),
            pltpu.SemaphoreType.DMA((ff // chunk(ff, 512),)),
        ],
        grant,
        cost(3, 2),
        {n: 4},
    )
    keep_rest, send_rest = call(
        functools.partial(rest_kernel, lead),
        [vmem(weights), vmem(grads), score],
        [shape((rows // 2, rest), BF)] * 2,
        [VMEM] * 3,
        limit=grant,
        cost=cost(1, 1),
    )
    send_rest, routes, w_router, tokens = lax.optimization_barrier((send_rest, routes, w_router, tokens))
    relative = (routes - lax.axis_index("expert")) % experts
    weight, sign, pair = call(
        route_kernel,
        [tokens, w_router, routes, relative],
        [shape((own, experts + 1), F32), shape((own, experts), F32), shape((own, experts), F32)],
        [VMEM] * 4,
        limit=small,
    )

    def collect(keep, send, tail):
        add = functools.partial(add_kernel, tail)
        total = keep.shape[1]
        for bit in bits[:0:-1]:
            arrived = across(send, bit)
            outs = [shape((keep.shape[0] // 2, total), BF)] * 2
            keep, send = call(add, [keep, arrived], outs, [VMEM] * 2, limit=small)
        arrived = across(send, bits[0])
        outs = [shape((own, total), BF)] * experts
        blocks = call(add, [keep, arrived], outs, [VMEM] * 2, limit=small)
        return [blocks[0]] + [along(blocks[s], experts - s) for s in range(1, experts)]

    first, second = collect(keep, send, False), collect(keep_rest, send_rest, True)
    input_grad, logit_grad = call(
        functools.partial(final_kernel, experts),
        first + second + [weight, sign, pair, w_router.astype(F32).T],
        [shape((own, width), BF), shape((own, 2), F32)],
        [VMEM] * (2 * experts + 4),
        limit=small,
    )
    return (input_grad, logit_grad)


def solution(mesh):
    row = P(("parts", "expert", "hidden"), None)
    placed = (
        row,
        row,
        row,
        P(),
        P("expert", None, "hidden"),
        P("expert", None, "hidden"),
        P("expert", "hidden", None),
    )
    return jax.shard_map(
        functools.partial(shards, mesh.shape["hidden"]),
        mesh=mesh,
        in_specs=placed,
        out_specs=(row, row),
        check_vma=False,
    )
```

```python
import functools

import jax
import jax.numpy as jnp
from jax import lax
from jax.experimental import pallas as pl
from jax.experimental.pallas import tpu as pltpu
from jax.sharding import PartitionSpec as P

BF = jnp.bfloat16
F32 = jnp.float32
LANES = 128
ROWS = 256
GRANT = 20 << 20
AHEAD = 2
NT = (((1,), (1,)), ((), ()))
ANY = pl.BlockSpec(memory_space=pl.ANY)
VMEM = pl.BlockSpec(memory_space=pltpu.VMEM)


def dot_nt(a, b):
    return lax.dot_general(a, b, NT, preferred_element_type=F32)


def chunk(extent, wanted):
    size = min(extent, wanted)
    while extent % size:
        size -= LANES
    return size


def pieces_of(extent):
    parts, at = [], 0
    while at < extent:
        size = min(512 if at < 1024 else 1024, extent - at)
        parts.append(pl.ds(at, size))
        at += size
    return parts


def fetch(pieces, held, sems):
    copies, at = [], 0
    for i, piece in enumerate(pieces):
        rows = piece.shape[0]
        copies.append(pltpu.make_async_copy(piece, held.at[pl.ds(at, rows)], sems.at[i]))
        at += rows
    for copy in copies:
        copy.start()
    for copy in copies:
        copy.wait()


def load_kernel(first, second, target, sems):
    copies = [pltpu.make_async_copy(w, target.at[i], sems.at[i]) for i, w in enumerate((first, second))]
    for copy in copies:
        copy.start()
    for copy in copies:
        copy.wait()


def gate_up_kernel(n, *refs):
    pieces, (weights, both, _, held, sems) = refs[:n], refs[n:]
    fetch(pieces, held, sems)
    rows, ff = both.shape[1:]
    block, step = min(rows, ROWS), chunk(ff, 1024)

    @pl.loop(0, rows // block)
    def _(r):
        at = pl.ds(pl.multiple_of(r * block, block), block)

        @pl.loop(0, ff // step)
        def _(f):
            cols = pl.ds(pl.multiple_of(f * step, step), step)
            for k in range(2):
                both[k, at, cols] = jnp.dot(held[at, :], weights[k, :, cols], preferred_element_type=F32)


def split3(score):
    high = score.astype(BF)
    rest = score - high.astype(F32)
    mid = rest.astype(BF)
    low = (rest - mid.astype(F32)).astype(BF)
    lane = lax.broadcasted_iota(jnp.int32, (score.shape[0], LANES), 1)
    spread = [jnp.broadcast_to(t.astype(F32), lane.shape) for t in (high, mid, low)]
    out = jnp.where(lane == 0, spread[0], jnp.where(lane == 1, spread[1], spread[2]))
    return jnp.where(lane < 3, out, 0.0).astype(BF)


def join3(tail):
    return jnp.sum(tail.astype(F32), axis=1, keepdims=True)


def store_halves(r, block, rows, cols, value, keep, send):
    half = rows // 2
    if rows == block:
        keep[:, cols] = value[:half]
        send[:, cols] = value[half:]
    else:

        @pl.when(r < half // block)
        def _():
            keep[pl.ds(pl.multiple_of(r * block, block), block), cols] = value

        @pl.when(r >= half // block)
        def _():
            send[pl.ds(pl.multiple_of(r * block - half, block), block), cols] = value


def sum_columns(start, width, r, block, grads, weights, keep, send):
    rows = grads.shape[1]
    at = pl.ds(pl.multiple_of(r * block, block), block)
    step = chunk(width, 1536)

    @pl.loop(0, width // step)
    def _(d):
        source = pl.ds(pl.multiple_of(start + d * step, step), step)
        cols = pl.ds(pl.multiple_of(d * step, step), step)
        value = dot_nt(grads[0, at, :], weights[0, source, :])
        value = value + dot_nt(grads[1, at, :], weights[1, source, :])
        store_halves(r, block, rows, cols, value.astype(BF), keep, send)


def back_kernel(n, *refs):
    pieces = refs[:n]
    weights, w_down, both, keep, send, grads, score, _, held, v_down, sems, down_sems = refs[n:]
    rows, ff = both.shape[1:]
    block = min(rows, ROWS)
    parts = pieces_of(ff)
    copies = [
        pltpu.make_async_copy(w_down.at[part], v_down.at[part], down_sems.at[i]) for i, part in enumerate(parts)
    ]
    copies[0].start()
    fetch(pieces, held, sems)
    for copy in copies[1:AHEAD]:
        copy.start()

    @pl.loop(0, rows // block)
    def _(r):
        at = pl.ds(pl.multiple_of(r * block, block), block)
        score[at, :] = jnp.zeros((block, 1), F32)

        for f, cols in enumerate(parts):

            @pl.when(r == 0)
            def _():
                copies[f].wait()
                if f + AHEAD < len(copies):
                    copies[f + AHEAD].start()

            back = dot_nt(held[at, :], v_down[cols, :])
            g, u = both[0, at, cols], both[1, at, cols]
            sig = jax.nn.sigmoid(g)
            silu = g * sig
            score[at, :] += jnp.sum(silu * u * back, axis=1, keepdims=True)
            grads[0, at, cols] = (back * u * sig * (1.0 + g * (1.0 - sig))).astype(BF)
            grads[1, at, cols] = (back * silu).astype(BF)

        sum_columns(0, keep.shape[1], r, block, grads, weights, keep, send)


def rest_kernel(start, weights, grads, score, keep, send):
    rows = grads.shape[1]
    width = keep.shape[1] - LANES
    block, half = min(rows, ROWS), rows // 2

    @pl.loop(0, rows // block)
    def _(r):
        sum_columns(start, width, r, block, grads, weights, keep, send)

    keep[:, pl.ds(width, LANES)] = split3(score[pl.ds(0, half), :])
    send[:, pl.ds(width, LANES)] = split3(score[pl.ds(half, half), :])


def add_kernel(tail, mine, theirs, *outs):
    width = mine.shape[1] - (LANES if tail else 0)
    at = 0
    for out in outs:
        rows = out.shape[0]
        here = pl.ds(at, rows)
        total = mine[here, pl.ds(0, width)].astype(F32) + theirs[here, pl.ds(0, width)].astype(F32)
        out[:, pl.ds(0, width)] = total.astype(BF)
        if tail:
            last = pl.ds(width, LANES)
            out[:, last] = split3(join3(mine[here, last]) + join3(theirs[here, last]))
        at += rows


def route_kernel(tokens, w_router, routes, relative, weight, sign, pair):
    experts = w_router.shape[0]
    logits = dot_nt(tokens[...], w_router[...])
    label = lax.broadcasted_iota(jnp.int32, logits.shape, 1)
    first, second = label == routes[:, 0:1], label == routes[:, 1:2]
    chosen = [jnp.sum(jnp.where(m, logits, 0.0), axis=1, keepdims=True) for m in (first, second)]
    prob = [jax.nn.sigmoid(chosen[0] - chosen[1]), jax.nn.sigmoid(chosen[1] - chosen[0])]
    pair[...] = jnp.where(first, 1.0, 0.0) - jnp.where(second, 1.0, 0.0)
    first, second = label == relative[:, 0:1], label == relative[:, 1:2]
    weight[:, pl.ds(0, experts)] = jnp.where(first, prob[0], 0.0) + jnp.where(second, prob[1], 0.0)
    weight[:, pl.ds(experts, 1)] = prob[0] * prob[1]
    sign[...] = jnp.where(first, 1.0, 0.0) - jnp.where(second, 1.0, 0.0)


def final_kernel(n, *refs):
    first, second, (weight, sign, pair, router, out, logit_grad) = refs[:n], refs[n : 2 * n], refs[2 * n :]
    lead = first[0].shape[1]
    gap = 0.0
    for s, block in enumerate(second):
        gap = gap + sign[:, s : s + 1] * join3(block[:, pl.ds(out.shape[1] - lead, LANES)])
    grad = weight[:, n : n + 1] * gap
    turned = jnp.broadcast_to(grad, (grad.shape[0], LANES)).T
    logit_grad[0:1, :] = turned[0:1, :]
    logit_grad[1:2, :] = -turned[0:1, :]
    for blocks, cols in ((first, pl.ds(0, lead)), (second, pl.ds(lead, out.shape[1] - lead))):
        total = 0.0
        for s, block in enumerate(blocks):
            total = total + weight[:, s : s + 1] * block[:, pl.ds(0, cols.size)].astype(F32)
        for e in range(n):
            total = total + (grad * pair[:, e : e + 1]) * router[e : e + 1, cols]
        out[:, cols] = total.astype(BF)


def call(kernel, args, outs, specs, scratch=(), limit=None, cost=None, alias={}):
    return pl.pallas_call(
        kernel,
        out_shape=outs,
        in_specs=specs,
        out_specs=[VMEM] * len(outs),
        scratch_shapes=list(scratch),
        compiler_params=pltpu.CompilerParams(vmem_limit_bytes=limit),
        cost_estimate=cost,
        input_output_aliases=alias,
    )(*args)


def shards(hidden, tokens, grad_out, routes, w_router, w_gate, w_up, w_down):
    own, width = tokens.shape
    experts = w_router.shape[1]
    ff = w_gate.shape[2]
    shape = jax.ShapeDtypeStruct
    bits = []
    while (1 << len(bits)) < hidden:
        bits.append(1 << len(bits))
    bits = bits[1:] + bits[:1]

    def along(x, shift):
        return lax.ppermute(x, "expert", [(i, i ^ shift) for i in range(experts)])

    def across(x, bit):
        return lax.ppermute(x, "hidden", [(i, i ^ bit) for i in range(hidden)])

    rows = own * experts * hidden
    macs = rows * width * ff
    lead = width // 2
    rest = width - lead + LANES
    resident_bytes = rows * (2 * width + 8 * LANES) + rows * (ff * 4 + lead * 2 + rest * 2)
    grant = GRANT if rows <= ROWS else resident_bytes + (14 << 20)
    small = min(rows, 2048) * (width + LANES) * 4 + (1 << 20)

    def cost(weights, matmuls):
        return pl.CostEstimate(
            flops=int(2 * matmuls * macs), bytes_accessed=2 * weights * width * ff, transcendentals=0
        )

    def vmem(x):
        return pltpu.with_memory_space_constraint(x, pltpu.VMEM)

    def hbm(x):
        return pltpu.with_memory_space_constraint(x, pltpu.HBM)

    def column(x):
        return jnp.concatenate([x] + [along(x, s) for s in range(1, experts)])

    def spread(pieces, some):
        for bit in some:
            pieces = pieces + [across(piece, bit) for piece in pieces]
        return pieces

    w_gate, w_up, w_down = [hbm(w[0]) for w in (w_gate, w_up, w_down)]
    held = pltpu.VMEM((rows, width), BF)
    pair_of = shape((2, *w_gate.shape), BF)
    (weights,) = call(
        load_kernel, [w_gate, w_up], [pair_of], [ANY] * 2, [pltpu.SemaphoreType.DMA((2,))], grant, cost(2, 0)
    )
    x_column, weights = lax.optimization_barrier((column(tokens), vmem(weights)))
    x_column, grad_out = lax.optimization_barrier((x_column, grad_out))
    x_pieces = spread([x_column], bits)
    dy_pieces = spread([column(grad_out)], bits[:-1])
    n = len(x_pieces)
    both, weights = call(
        functools.partial(gate_up_kernel, n),
        x_pieces + [weights],
        [shape((2, rows, ff), F32), pair_of],
        [ANY] * n + [VMEM],
        [held, pltpu.SemaphoreType.DMA((n,))],
        grant,
        cost(2, 2),
        {n: 1},
    )
    both, weights = vmem(both), vmem(weights)
    *late, both = lax.optimization_barrier((*dy_pieces[1:], both))
    dy_pieces = spread(dy_pieces[:1] + late, bits[-1:])
    keep, send, grads, score, weights = call(
        functools.partial(back_kernel, n),
        dy_pieces + [weights, w_down, both],
        [shape((rows // 2, lead), BF)] * 2 + [shape((2, rows, ff), BF), shape((rows, 1), F32), pair_of],
        [ANY] * n + [VMEM, ANY, VMEM],
        [
            held,
            pltpu.VMEM((ff, width), BF),
            pltpu.SemaphoreType.DMA((n,)),
            pltpu.SemaphoreType.DMA((len(pieces_of(ff)),)),
        ],
        grant,
        cost(3, 2),
        {n: 4},
    )
    keep_rest, send_rest = call(
        functools.partial(rest_kernel, lead),
        [vmem(weights), vmem(grads), score],
        [shape((rows // 2, rest), BF)] * 2,
        [VMEM] * 3,
        limit=grant,
        cost=cost(1, 1),
    )
    send_rest, routes, w_router, tokens = lax.optimization_barrier((send_rest, routes, w_router, tokens))
    relative = routes ^ lax.axis_index("expert")
    weight, sign, pair = call(
        route_kernel,
        [tokens, w_router.T, routes, relative],
        [shape((own, experts + 1), F32), shape((own, experts), F32), shape((own, experts), F32)],
        [VMEM] * 4,
        limit=small,
    )

    def collect(keep, send, tail):
        add = functools.partial(add_kernel, tail)
        total = keep.shape[1]
        for bit in bits[:0:-1]:
            arrived = across(send, bit)
            outs = [shape((keep.shape[0] // 2, total), BF)] * 2
            keep, send = call(add, [keep, arrived], outs, [VMEM] * 2, limit=small)
        arrived = across(send, bits[0])
        outs = [shape((own, total), BF)] * experts
        blocks = call(add, [keep, arrived], outs, [VMEM] * 2, limit=small)
        return [blocks[0]] + [along(blocks[s], s) for s in range(1, experts)]

    first, second = collect(keep, send, False), collect(keep_rest, send_rest, True)
    input_grad, logit_grad = call(
        functools.partial(final_kernel, experts),
        first + second + [weight, sign, pair, w_router.astype(F32).T],
        [shape((own, width), BF), shape((2, own), F32)],
        [VMEM] * (2 * experts + 4),
        limit=small,
    )
    return (input_grad, logit_grad.T)


def solution(mesh):
    row = P(("parts", "expert", "hidden"), None)
    placed = (
        row,
        row,
        row,
        P(),
        P("expert", None, "hidden"),
        P("expert", None, "hidden"),
        P("expert", "hidden", None),
    )
    return jax.shard_map(
        functools.partial(shards, mesh.shape["hidden"]),
        mesh=mesh,
        in_specs=placed,
        out_specs=(row, row),
        check_vma=False,
    )
```

```python
import functools

import jax
import jax.numpy as jnp
from jax import lax
from jax.experimental import pallas as pl
from jax.experimental.pallas import tpu as pltpu
from jax.sharding import PartitionSpec as P

BF = jnp.bfloat16
F32 = jnp.float32
LANES = 128
ROWS = 256
GRANT = 15 << 20
NT = (((1,), (1,)), ((), ()))
ANY = pl.BlockSpec(memory_space=pl.ANY)
VMEM = pl.BlockSpec(memory_space=pltpu.VMEM)


def dot_nt(a, b):
    return lax.dot_general(a, b, NT, preferred_element_type=F32)


def chunk(extent, wanted):
    size = min(extent, wanted)
    while extent % size:
        size -= LANES
    return size


def fetch(pieces, held, sems):
    copies, at = [], 0
    for i, piece in enumerate(pieces):
        rows = piece.shape[0]
        copies.append(pltpu.make_async_copy(piece, held.at[pl.ds(at, rows)], sems.at[i]))
        at += rows
    for copy in copies:
        copy.start()
    for copy in copies:
        copy.wait()


def load_kernel(k, source, *refs):
    copy = pltpu.make_async_copy(source, refs[-2].at[k], refs[-1])
    copy.start()
    copy.wait()


def gate_up_kernel(n, *refs):
    pieces, (weights, w_down, both, _, near_down, held, sems) = refs[:n], refs[n:]
    copy = pltpu.make_async_copy(w_down.at[pl.ds(0, near_down.shape[0])], near_down, sems.at[n])
    copy.start()
    fetch(pieces, held, sems)
    rows, ff = both.shape[1:]
    block, step = min(rows, ROWS), chunk(ff, 1024)

    @pl.loop(0, rows // block)
    def _(r):
        at = pl.ds(pl.multiple_of(r * block, block), block)

        @pl.loop(0, ff // step)
        def _(f):
            cols = pl.ds(pl.multiple_of(f * step, step), step)
            for k in range(2):
                both[k, at, cols] = jnp.dot(held[at, :], weights[k, :, cols], preferred_element_type=F32)

    copy.wait()


def split3(score):
    high = score.astype(BF)
    rest = score - high.astype(F32)
    mid = rest.astype(BF)
    low = (rest - mid.astype(F32)).astype(BF)
    lane = lax.broadcasted_iota(jnp.int32, (score.shape[0], LANES), 1)
    spread = [jnp.broadcast_to(t.astype(F32), lane.shape) for t in (high, mid, low)]
    out = jnp.where(lane == 0, spread[0], jnp.where(lane == 1, spread[1], spread[2]))
    return jnp.where(lane < 3, out, 0.0).astype(BF)


def join3(tail):
    return jnp.sum(tail.astype(F32), axis=1, keepdims=True)


def store_halves(r, block, rows, cols, value, keep, send):
    half = rows // 2
    if rows == block:
        keep[:, cols] = value[:half]
        send[:, cols] = value[half:]
    else:

        @pl.when(r < half // block)
        def _():
            keep[pl.ds(pl.multiple_of(r * block, block), block), cols] = value

        @pl.when(r >= half // block)
        def _():
            send[pl.ds(pl.multiple_of(r * block - half, block), block), cols] = value


def sum_columns(start, width, r, block, grads, weights, keep, send):
    rows = grads.shape[1]
    at = pl.ds(pl.multiple_of(r * block, block), block)
    step = chunk(width, 1536)

    @pl.loop(0, width // step)
    def _(d):
        source = pl.ds(pl.multiple_of(start + d * step, step), step)
        cols = pl.ds(pl.multiple_of(d * step, step), step)
        value = dot_nt(grads[0, at, :], weights[0, source, :])
        value = value + dot_nt(grads[1, at, :], weights[1, source, :])
        store_halves(r, block, rows, cols, value.astype(BF), keep, send)


def back_kernel(n, *refs):
    pieces = refs[:n]
    weights, w_down, near_down, both, keep, send, grads, score, _, held, v_down, sem, sems = refs[n:]
    rows, ff = both.shape[1:]
    block = min(rows, ROWS)
    near = near_down.shape[0]
    step = chunk(near, 1024)
    copy = pltpu.make_async_copy(w_down.at[pl.ds(near, ff - near)], v_down, sem)
    copy.start()
    fetch(pieces, held, sems)

    @pl.loop(0, rows // block)
    def _(r):
        at = pl.ds(pl.multiple_of(r * block, block), block)
        score[at, :] = jnp.zeros((block, 1), F32)

        for f in range(ff // step):
            cols = pl.ds(f * step, step)
            if f * step == near:

                @pl.when(r == 0)
                def _():
                    copy.wait()

            down = near_down[cols, :] if f * step < near else v_down[pl.ds(f * step - near, step), :]
            back = dot_nt(held[at, :], down)
            g, u = both[0, at, cols], both[1, at, cols]
            sig = jax.nn.sigmoid(g)
            silu = g * sig
            score[at, :] += jnp.sum(silu * u * back, axis=1, keepdims=True)
            grads[0, at, cols] = (back * u * sig * (1.0 + g * (1.0 - sig))).astype(BF)
            grads[1, at, cols] = (back * silu).astype(BF)

        sum_columns(0, keep.shape[1], r, block, grads, weights, keep, send)


def rest_kernel(start, weights, grads, score, keep, send):
    rows = grads.shape[1]
    width = keep.shape[1] - LANES
    block, half = min(rows, ROWS), rows // 2

    @pl.loop(0, rows // block)
    def _(r):
        sum_columns(start, width, r, block, grads, weights, keep, send)

    keep[:, pl.ds(width, LANES)] = split3(score[pl.ds(0, half), :])
    send[:, pl.ds(width, LANES)] = split3(score[pl.ds(half, half), :])


def add_kernel(tail, mine, theirs, *outs):
    width = mine.shape[1] - (LANES if tail else 0)
    at = 0
    for out in outs:
        rows = out.shape[0]
        here = pl.ds(at, rows)
        total = mine[here, pl.ds(0, width)].astype(F32) + theirs[here, pl.ds(0, width)].astype(F32)
        out[:, pl.ds(0, width)] = total.astype(BF)
        if tail:
            last = pl.ds(width, LANES)
            out[:, last] = split3(join3(mine[here, last]) + join3(theirs[here, last]))
        at += rows


def route_kernel(tokens, w_router, routes, relative, weight, sign, pair):
    experts = w_router.shape[0]
    logits = dot_nt(tokens[...], w_router[...])
    label = lax.broadcasted_iota(jnp.int32, logits.shape, 1)
    first, second = label == routes[:, 0:1], label == routes[:, 1:2]
    chosen = [jnp.sum(jnp.where(m, logits, 0.0), axis=1, keepdims=True) for m in (first, second)]
    prob = [jax.nn.sigmoid(chosen[0] - chosen[1]), jax.nn.sigmoid(chosen[1] - chosen[0])]
    pair[...] = jnp.where(first, 1.0, 0.0) - jnp.where(second, 1.0, 0.0)
    first, second = label == relative[:, 0:1], label == relative[:, 1:2]
    weight[:, pl.ds(0, experts)] = jnp.where(first, prob[0], 0.0) + jnp.where(second, prob[1], 0.0)
    weight[:, pl.ds(experts, 1)] = prob[0] * prob[1]
    sign[...] = jnp.where(first, 1.0, 0.0) - jnp.where(second, 1.0, 0.0)


def final_kernel(n, *refs):
    first, second, (weight, sign, pair, router, out, logit_grad) = refs[:n], refs[n : 2 * n], refs[2 * n :]
    lead = first[0].shape[1]
    gap = 0.0
    for s, block in enumerate(second):
        gap = gap + sign[:, s : s + 1] * join3(block[:, pl.ds(out.shape[1] - lead, LANES)])
    grad = weight[:, n : n + 1] * gap
    turned = jnp.broadcast_to(grad, (grad.shape[0], LANES)).T
    logit_grad[0:1, :] = turned[0:1, :]
    logit_grad[1:2, :] = -turned[0:1, :]
    for blocks, cols in ((first, pl.ds(0, lead)), (second, pl.ds(lead, out.shape[1] - lead))):
        total = 0.0
        for s, block in enumerate(blocks):
            total = total + weight[:, s : s + 1] * block[:, pl.ds(0, cols.size)].astype(F32)
        for e in range(n):
            total = total + (grad * pair[:, e : e + 1]) * router[e : e + 1, cols]
        out[:, cols] = total.astype(BF)


def call(kernel, args, outs, specs, scratch=(), limit=None, cost=None, alias={}):
    return pl.pallas_call(
        kernel,
        out_shape=outs,
        in_specs=specs,
        out_specs=[VMEM] * len(outs),
        scratch_shapes=list(scratch),
        compiler_params=pltpu.CompilerParams(vmem_limit_bytes=limit),
        cost_estimate=cost,
        input_output_aliases=alias,
    )(*args)


def shards(hidden, tokens, grad_out, routes, w_router, w_gate, w_up, w_down):
    own, width = tokens.shape
    experts = w_router.shape[1]
    ff = w_gate.shape[2]
    shape = jax.ShapeDtypeStruct
    bits = []
    while (1 << len(bits)) < hidden:
        bits.append(1 << len(bits))
    bits = bits[1:] + bits[:1]

    def along(x, shift):
        return lax.ppermute(x, "expert", [(i, i ^ shift) for i in range(experts)])

    def across(x, bit):
        return lax.ppermute(x, "hidden", [(i, i ^ bit) for i in range(hidden)])

    rows = own * experts * hidden
    macs = rows * width * ff
    lead = width // 2
    rest = width - lead + LANES
    resident_bytes = rows * (2 * width + 8 * LANES) + rows * (ff * 4 + lead * 2 + rest * 2)
    grant = GRANT if rows <= ROWS else resident_bytes + (14 << 20)
    small = min(rows, 2048) * (width + LANES) * 4 + (1 << 20)

    def cost(weights, matmuls):
        return pl.CostEstimate(
            flops=int(2 * matmuls * macs), bytes_accessed=2 * weights * width * ff, transcendentals=0
        )

    def vmem(x):
        return pltpu.with_memory_space_constraint(x, pltpu.VMEM)

    def hbm(x):
        return pltpu.with_memory_space_constraint(x, pltpu.HBM)

    def column(x):
        return jnp.concatenate([x] + [along(x, s) for s in range(1, experts)])

    def spread(pieces, some):
        for bit in some:
            pieces = pieces + [across(piece, bit) for piece in pieces]
        return pieces

    w_gate, w_up, w_down = [hbm(w[0]) for w in (w_gate, w_up, w_down)]
    held = pltpu.VMEM((rows, width), BF)
    pair_of = shape((2, *w_gate.shape), BF)
    def load(k, *args):
        specs = [ANY, VMEM][: len(args)]
        alias = {1: 0} if k else {}
        sem = [pltpu.SemaphoreType.DMA]
        (out,) = call(functools.partial(load_kernel, k), args, [pair_of], specs, sem, grant, cost(0, 0), alias)
        return vmem(out)

    x_column, weights = lax.optimization_barrier((column(tokens), load(0, w_gate)))
    x_pieces = spread([x_column], bits[:-1])
    x_pieces[-1], weights = lax.optimization_barrier((x_pieces[-1], load(1, w_up, weights)))
    x_pieces = spread(x_pieces, bits[-1:])
    dy_pieces = spread([column(grad_out)], [bit ^ bits[-1] for bit in bits[:-1]])
    n = len(x_pieces)
    both, weights, near_down = call(
        functools.partial(gate_up_kernel, n),
        x_pieces + [weights, w_down],
        [shape((2, rows, ff), F32), pair_of, shape((ff // 2, width), BF)],
        [ANY] * n + [VMEM, ANY],
        [held, pltpu.SemaphoreType.DMA((n + 1,))],
        grant,
        cost(2, 2),
        {n: 1},
    )
    both, weights, near_down = vmem(both), vmem(weights), vmem(near_down)
    *late, both = lax.optimization_barrier((*dy_pieces[1:], both))
    dy_pieces = spread(dy_pieces[:1] + late, bits[-1:])
    half = len(dy_pieces) // 2
    turned = [bin(i).count("1") % 2 for i in range(half)]
    order = [i + half * turned[i] for i in range(half)] + [i + half - half * turned[i] for i in range(half)]
    dy_pieces = [dy_pieces[i] for i in order]
    keep, send, grads, score, weights = call(
        functools.partial(back_kernel, n),
        dy_pieces + [weights, w_down, near_down, both],
        [shape((rows // 2, lead), BF)] * 2 + [shape((2, rows, ff), BF), shape((rows, 1), F32), pair_of],
        [ANY] * n + [VMEM, ANY, VMEM, VMEM],
        [
            held,
            pltpu.VMEM((ff - ff // 2, width), BF),
            pltpu.SemaphoreType.DMA,
            pltpu.SemaphoreType.DMA((n,)),
        ],
        grant,
        cost(3, 2),
        {n: 4},
    )
    keep_rest, send_rest = call(
        functools.partial(rest_kernel, lead),
        [vmem(weights), vmem(grads), score],
        [shape((rows // 2, rest), BF)] * 2,
        [VMEM] * 3,
        limit=grant,
        cost=cost(1, 1),
    )
    send_rest, routes, w_router, tokens = lax.optimization_barrier((send_rest, routes, w_router, tokens))
    relative = routes ^ lax.axis_index("expert")
    weight, sign, pair = call(
        route_kernel,
        [tokens, w_router.T, routes, relative],
        [shape((own, experts + 1), F32), shape((own, experts), F32), shape((own, experts), F32)],
        [VMEM] * 4,
        limit=small,
    )

    def collect(keep, send, tail):
        add = functools.partial(add_kernel, tail)
        total = keep.shape[1]
        for bit in bits[:0:-1]:
            arrived = across(send, bit)
            outs = [shape((keep.shape[0] // 2, total), BF)] * 2
            keep, send = call(add, [keep, arrived], outs, [VMEM] * 2, limit=small)
        arrived = across(send, bits[0])
        outs = [shape((own, total), BF)] * experts
        blocks = call(add, [keep, arrived], outs, [VMEM] * 2, limit=small)
        return [blocks[0]] + [along(blocks[s], s) for s in range(1, experts)]

    first, second = collect(keep, send, False), collect(keep_rest, send_rest, True)
    input_grad, logit_grad = call(
        functools.partial(final_kernel, experts),
        first + second + [weight, sign, pair, w_router.astype(F32).T],
        [shape((own, width), BF), shape((2, own), F32)],
        [VMEM] * (2 * experts + 4),
        limit=small,
    )
    return (input_grad, logit_grad.T)


def solution(mesh):
    row = P(("parts", "expert", "hidden"), None)
    placed = (
        row,
        row,
        row,
        P(),
        P("expert", None, "hidden"),
        P("expert", None, "hidden"),
        P("expert", "hidden", None),
    )
    return jax.shard_map(
        functools.partial(shards, mesh.shape["hidden"]),
        mesh=mesh,
        in_specs=placed,
        out_specs=(row, row),
        check_vma=False,
    )
```

```python
import functools

import jax
import jax.numpy as jnp
from jax import lax
from jax.experimental import pallas as pl
from jax.experimental.pallas import tpu as pltpu
from jax.sharding import PartitionSpec as P

BF = jnp.bfloat16
F32 = jnp.float32
LANES = 128
ROWS = 256
GRANT = 15 << 20
NT = (((1,), (1,)), ((), ()))
ANY = pl.BlockSpec(memory_space=pl.ANY)
VMEM = pl.BlockSpec(memory_space=pltpu.VMEM)


def dot_nt(a, b):
    return lax.dot_general(a, b, NT, preferred_element_type=F32)


def chunk(extent, wanted):
    size = min(extent, wanted)
    while extent % size:
        size -= LANES
    return size


def fetch(pieces, held, sems):
    copies, at = [], 0
    for i, piece in enumerate(pieces):
        rows = piece.shape[0]
        copies.append(pltpu.make_async_copy(piece, held.at[pl.ds(at, rows)], sems.at[i]))
        at += rows
    for copy in copies:
        copy.start()
    for copy in copies:
        copy.wait()


def load_kernel(k, source, *refs):
    copy = pltpu.make_async_copy(source, refs[-2].at[k], refs[-1])
    copy.start()
    copy.wait()


def gate_up_kernel(n, *refs):
    pieces, (weights, w_down, both, _, near_down, held, sems) = refs[:n], refs[n:]
    copy = pltpu.make_async_copy(w_down.at[pl.ds(0, near_down.shape[0])], near_down, sems.at[n])
    copy.start()
    fetch(pieces, held, sems)
    rows, ff = both.shape[1:]
    block, step = min(rows, ROWS), chunk(ff, 1024)

    @pl.loop(0, rows // block)
    def _(r):
        at = pl.ds(pl.multiple_of(r * block, block), block)

        @pl.loop(0, ff // step)
        def _(f):
            cols = pl.ds(pl.multiple_of(f * step, step), step)
            for k in range(2):
                both[k, at, cols] = jnp.dot(held[at, :], weights[k, :, cols], preferred_element_type=F32)

    copy.wait()


def split3(score):
    high = score.astype(BF)
    rest = score - high.astype(F32)
    mid = rest.astype(BF)
    low = (rest - mid.astype(F32)).astype(BF)
    lane = lax.broadcasted_iota(jnp.int32, (score.shape[0], LANES), 1)
    spread = [jnp.broadcast_to(t.astype(F32), lane.shape) for t in (high, mid, low)]
    out = jnp.where(lane == 0, spread[0], jnp.where(lane == 1, spread[1], spread[2]))
    return jnp.where(lane < 3, out, 0.0).astype(BF)


def join3(tail):
    return jnp.sum(tail.astype(F32), axis=1, keepdims=True)


def store_halves(r, block, rows, cols, value, keep, send):
    half = rows // 2
    if rows == block:
        keep[:, cols] = value[:half]
        send[:, cols] = value[half:].astype(BF)
    else:

        @pl.when(r < half // block)
        def _():
            keep[pl.ds(pl.multiple_of(r * block, block), block), cols] = value

        @pl.when(r >= half // block)
        def _():
            send[pl.ds(pl.multiple_of(r * block - half, block), block), cols] = value.astype(BF)


def sum_columns(start, width, r, block, grads, weights, keep, send):
    rows = grads.shape[1]
    at = pl.ds(pl.multiple_of(r * block, block), block)
    step = chunk(width, 1536)

    @pl.loop(0, width // step)
    def _(d):
        source = pl.ds(pl.multiple_of(start + d * step, step), step)
        cols = pl.ds(pl.multiple_of(d * step, step), step)
        value = dot_nt(grads[0, at, :], weights[0, source, :])
        value = value + dot_nt(grads[1, at, :], weights[1, source, :])
        store_halves(r, block, rows, cols, value, keep, send)


def back_kernel(n, *refs):
    pieces = refs[:n]
    weights, w_down, near_down, both, keep, send, grads, score, _, held, v_down, sem, sems = refs[n:]
    rows, ff = both.shape[1:]
    block = min(rows, ROWS)
    near = near_down.shape[0]
    step = chunk(near, 1024)
    copy = pltpu.make_async_copy(w_down.at[pl.ds(near, ff - near)], v_down, sem)
    copy.start()
    fetch(pieces, held, sems)

    @pl.loop(0, rows // block)
    def _(r):
        at = pl.ds(pl.multiple_of(r * block, block), block)
        score[at, :] = jnp.zeros((block, 1), F32)

        for f in range(ff // step):
            cols = pl.ds(f * step, step)
            if f * step == near:

                @pl.when(r == 0)
                def _():
                    copy.wait()

            down = near_down[cols, :] if f * step < near else v_down[pl.ds(f * step - near, step), :]
            back = dot_nt(held[at, :], down)
            g, u = both[0, at, cols], both[1, at, cols]
            sig = jax.nn.sigmoid(g)
            silu = g * sig
            score[at, :] += jnp.sum(silu * u * back, axis=1, keepdims=True)
            grads[0, at, cols] = (back * u * sig * (1.0 + g * (1.0 - sig))).astype(BF)
            grads[1, at, cols] = (back * silu).astype(BF)

        sum_columns(0, keep.shape[1], r, block, grads, weights, keep, send)


def rest_kernel(start, weights, grads, score, keep, send):
    rows = grads.shape[1]
    width = keep.shape[1] - LANES
    block, half = min(rows, ROWS), rows // 2

    @pl.loop(0, rows // block)
    def _(r):
        sum_columns(start, width, r, block, grads, weights, keep, send)

    keep[:, pl.ds(width, LANES)] = split3(score[pl.ds(0, half), :]).astype(F32)
    send[:, pl.ds(width, LANES)] = split3(score[pl.ds(half, half), :])


def add_kernel(tail, mine, theirs, *outs):
    width = mine.shape[1] - (LANES if tail else 0)
    at = 0
    for out in outs:
        rows = out.shape[0]
        here = pl.ds(at, rows)
        total = mine[here, pl.ds(0, width)] + theirs[here, pl.ds(0, width)].astype(F32)
        out[:, pl.ds(0, width)] = total.astype(out.dtype)
        if tail:
            last = pl.ds(width, LANES)
            out[:, last] = split3(join3(mine[here, last]) + join3(theirs[here, last])).astype(out.dtype)
        at += rows


def route_kernel(tokens, w_router, routes, relative, weight, sign, pair):
    experts = w_router.shape[0]
    logits = dot_nt(tokens[...], w_router[...])
    label = lax.broadcasted_iota(jnp.int32, logits.shape, 1)
    first, second = label == routes[:, 0:1], label == routes[:, 1:2]
    chosen = [jnp.sum(jnp.where(m, logits, 0.0), axis=1, keepdims=True) for m in (first, second)]
    prob = [jax.nn.sigmoid(chosen[0] - chosen[1]), jax.nn.sigmoid(chosen[1] - chosen[0])]
    pair[...] = jnp.where(first, 1.0, 0.0) - jnp.where(second, 1.0, 0.0)
    first, second = label == relative[:, 0:1], label == relative[:, 1:2]
    weight[:, pl.ds(0, experts)] = jnp.where(first, prob[0], 0.0) + jnp.where(second, prob[1], 0.0)
    weight[:, pl.ds(experts, 1)] = prob[0] * prob[1]
    sign[...] = jnp.where(first, 1.0, 0.0) - jnp.where(second, 1.0, 0.0)


def final_kernel(n, *refs):
    first, second, (weight, sign, pair, router, out, logit_grad) = refs[:n], refs[n : 2 * n], refs[2 * n :]
    lead = first[0].shape[1]
    gap = 0.0
    for s, block in enumerate(second):
        gap = gap + sign[:, s : s + 1] * join3(block[:, pl.ds(out.shape[1] - lead, LANES)])
    grad = weight[:, n : n + 1] * gap
    turned = jnp.broadcast_to(grad, (grad.shape[0], LANES)).T
    logit_grad[0:1, :] = turned[0:1, :]
    logit_grad[1:2, :] = -turned[0:1, :]
    for blocks, cols in ((first, pl.ds(0, lead)), (second, pl.ds(lead, out.shape[1] - lead))):
        total = 0.0
        for s, block in enumerate(blocks):
            total = total + weight[:, s : s + 1] * block[:, pl.ds(0, cols.size)].astype(F32)
        for e in range(n):
            total = total + (grad * pair[:, e : e + 1]) * router[e : e + 1, cols]
        out[:, cols] = total.astype(BF)


def call(kernel, args, outs, specs, scratch=(), limit=None, cost=None, alias={}):
    return pl.pallas_call(
        kernel,
        out_shape=outs,
        in_specs=specs,
        out_specs=[VMEM] * len(outs),
        scratch_shapes=list(scratch),
        compiler_params=pltpu.CompilerParams(vmem_limit_bytes=limit),
        cost_estimate=cost,
        input_output_aliases=alias,
    )(*args)


def shards(hidden, tokens, grad_out, routes, w_router, w_gate, w_up, w_down):
    own, width = tokens.shape
    experts = w_router.shape[1]
    ff = w_gate.shape[2]
    shape = jax.ShapeDtypeStruct
    bits = []
    while (1 << len(bits)) < hidden:
        bits.append(1 << len(bits))
    bits = bits[1:] + bits[:1]

    def along(x, shift):
        return lax.ppermute(x, "expert", [(i, i ^ shift) for i in range(experts)])

    def across(x, bit):
        return lax.ppermute(x, "hidden", [(i, i ^ bit) for i in range(hidden)])

    rows = own * experts * hidden
    macs = rows * width * ff
    lead = width // 2
    rest = width - lead + LANES
    resident_bytes = rows * (2 * width + 8 * LANES) + rows * (ff * 4 + lead * 3 + rest * 3)
    grant = GRANT if rows <= ROWS else resident_bytes + (8 << 20)
    small = min(rows, 2048) * (width + LANES) * 4 + (1 << 20)

    def cost(weights, matmuls):
        return pl.CostEstimate(
            flops=int(2 * matmuls * macs), bytes_accessed=2 * weights * width * ff, transcendentals=0
        )

    def vmem(x):
        return pltpu.with_memory_space_constraint(x, pltpu.VMEM)

    def hbm(x):
        return pltpu.with_memory_space_constraint(x, pltpu.HBM)

    def column(x):
        return jnp.concatenate([x] + [along(x, s) for s in range(1, experts)])

    def spread(pieces, some):
        for bit in some:
            pieces = pieces + [across(piece, bit) for piece in pieces]
        return pieces

    w_gate, w_up, w_down = [hbm(w[0]) for w in (w_gate, w_up, w_down)]
    held = pltpu.VMEM((rows, width), BF)
    pair_of = shape((2, *w_gate.shape), BF)
    def load(k, *args):
        specs = [ANY, VMEM][: len(args)]
        alias = {1: 0} if k else {}
        sem = [pltpu.SemaphoreType.DMA]
        (out,) = call(functools.partial(load_kernel, k), args, [pair_of], specs, sem, grant, cost(0, 0), alias)
        return vmem(out)

    x_column, weights = lax.optimization_barrier((column(tokens), load(0, w_gate)))
    x_pieces = spread([x_column], bits[:-1])
    x_pieces[-1], weights = lax.optimization_barrier((x_pieces[-1], load(1, w_up, weights)))
    x_pieces = spread(x_pieces, bits[-1:])
    dy_pieces = spread([column(grad_out)], [bit ^ bits[-1] for bit in bits[:-1]])
    n = len(x_pieces)
    both, weights, near_down = call(
        functools.partial(gate_up_kernel, n),
        x_pieces + [weights, w_down],
        [shape((2, rows, ff), F32), pair_of, shape((ff // 2, width), BF)],
        [ANY] * n + [VMEM, ANY],
        [held, pltpu.SemaphoreType.DMA((n + 1,))],
        grant,
        cost(2, 2),
        {n: 1},
    )
    both, weights, near_down = vmem(both), vmem(weights), vmem(near_down)
    *late, both = lax.optimization_barrier((*dy_pieces[1:], both))
    dy_pieces = spread(dy_pieces[:1] + late, bits[-1:])
    half = len(dy_pieces) // 2
    turned = [bin(i).count("1") % 2 for i in range(half)]
    order = [i + half * turned[i] for i in range(half)] + [i + half - half * turned[i] for i in range(half)]
    dy_pieces = [dy_pieces[i] for i in order]
    keep, send, grads, score, weights = call(
        functools.partial(back_kernel, n),
        dy_pieces + [weights, w_down, near_down, both],
        [shape((rows // 2, lead), F32), shape((rows // 2, lead), BF)]
        + [shape((2, rows, ff), BF), shape((rows, 1), F32), pair_of],
        [ANY] * n + [VMEM, ANY, VMEM, VMEM],
        [
            held,
            pltpu.VMEM((ff - ff // 2, width), BF),
            pltpu.SemaphoreType.DMA,
            pltpu.SemaphoreType.DMA((n,)),
        ],
        grant,
        cost(3, 2),
        {n: 4},
    )
    keep_rest, send_rest = call(
        functools.partial(rest_kernel, lead),
        [vmem(weights), vmem(grads), score],
        [shape((rows // 2, rest), F32), shape((rows // 2, rest), BF)],
        [VMEM] * 3,
        limit=grant,
        cost=cost(1, 1),
    )
    send_rest, routes, w_router, tokens = lax.optimization_barrier((send_rest, routes, w_router, tokens))
    relative = routes ^ lax.axis_index("expert")
    weight, sign, pair = call(
        route_kernel,
        [tokens, w_router.T, routes, relative],
        [shape((own, experts + 1), F32), shape((own, experts), F32), shape((own, experts), F32)],
        [VMEM] * 4,
        limit=small,
    )

    def collect(keep, send, tail):
        add = functools.partial(add_kernel, tail)
        total = keep.shape[1]
        for bit in bits[:0:-1]:
            arrived = across(send, bit)
            outs = [shape((keep.shape[0] // 2, total), kind) for kind in (F32, BF)]
            keep, send = call(add, [keep, arrived], outs, [VMEM] * 2, limit=small)
        arrived = across(send, bits[0])
        outs = [shape((own, total), F32)] + [shape((own, total), BF)] * (experts - 1)
        blocks = call(add, [keep, arrived], outs, [VMEM] * 2, limit=small)
        return [blocks[0]] + [along(blocks[s], s) for s in range(1, experts)]

    first, second = collect(keep, send, False), collect(keep_rest, send_rest, True)
    input_grad, logit_grad = call(
        functools.partial(final_kernel, experts),
        first + second + [weight, sign, pair, w_router.astype(F32).T],
        [shape((own, width), BF), shape((2, own), F32)],
        [VMEM] * (2 * experts + 4),
        limit=small,
    )
    return (input_grad, logit_grad.T)


def solution(mesh):
    row = P(("parts", "expert", "hidden"), None)
    placed = (
        row,
        row,
        row,
        P(),
        P("expert", None, "hidden"),
        P("expert", None, "hidden"),
        P("expert", "hidden", None),
    )
    return jax.shard_map(
        functools.partial(shards, mesh.shape["hidden"]),
        mesh=mesh,
        in_specs=placed,
        out_specs=(row, row),
        check_vma=False,
    )
```

```python
import functools

import jax
import jax.numpy as jnp
from jax import lax
from jax.experimental import pallas as pl
from jax.experimental.pallas import tpu as pltpu
from jax.sharding import PartitionSpec as P

BF = jnp.bfloat16
F32 = jnp.float32
LANES = 128
ROWS = 256
GRANT = 15 << 20
NT = (((1,), (1,)), ((), ()))
ANY = pl.BlockSpec(memory_space=pl.ANY)
VMEM = pl.BlockSpec(memory_space=pltpu.VMEM)


def dot_nt(a, b):
    return lax.dot_general(a, b, NT, preferred_element_type=F32)


def chunk(extent, wanted):
    size = min(extent, wanted)
    while extent % size:
        size -= LANES
    return size


def fetch(pieces, held, sems):
    copies, at = [], 0
    for i, piece in enumerate(pieces):
        rows = piece.shape[0]
        copies.append(pltpu.make_async_copy(piece, held.at[pl.ds(at, rows)], sems.at[i]))
        at += rows
    for copy in copies:
        copy.start()
    for copy in copies:
        copy.wait()


def load_kernel(k, source, *refs):
    copy = pltpu.make_async_copy(source, refs[-2].at[k], refs[-1])
    copy.start()
    copy.wait()


def gate_up_kernel(n, *refs):
    pieces, (weights, w_down, both, _, near_down, held, sems) = refs[:n], refs[n:]
    copy = pltpu.make_async_copy(w_down.at[pl.ds(0, near_down.shape[0])], near_down, sems.at[n])
    copy.start()
    fetch(pieces, held, sems)
    rows, ff = both.shape[1:]
    block, step = min(rows, ROWS), chunk(ff, 1024)

    @pl.loop(0, rows // block)
    def _(r):
        at = pl.ds(pl.multiple_of(r * block, block), block)

        @pl.loop(0, ff // step)
        def _(f):
            cols = pl.ds(pl.multiple_of(f * step, step), step)
            for k in range(2):
                both[k, at, cols] = jnp.dot(held[at, :], weights[k, :, cols], preferred_element_type=F32)

    copy.wait()


def split3(score):
    high = score.astype(BF)
    rest = score - high.astype(F32)
    mid = rest.astype(BF)
    low = (rest - mid.astype(F32)).astype(BF)
    lane = lax.broadcasted_iota(jnp.int32, (score.shape[0], LANES), 1)
    spread = [jnp.broadcast_to(t.astype(F32), lane.shape) for t in (high, mid, low)]
    out = jnp.where(lane == 0, spread[0], jnp.where(lane == 1, spread[1], spread[2]))
    return jnp.where(lane < 3, out, 0.0).astype(BF)


def join3(tail):
    return jnp.sum(tail.astype(F32), axis=1, keepdims=True)


def store_halves(r, block, rows, cols, value, keep, send):
    half = rows // 2
    if rows == block:
        keep[:, cols] = value[:half]
        send[:, cols] = value[half:].astype(BF)
    else:

        @pl.when(r < half // block)
        def _():
            keep[pl.ds(pl.multiple_of(r * block, block), block), cols] = value

        @pl.when(r >= half // block)
        def _():
            send[pl.ds(pl.multiple_of(r * block - half, block), block), cols] = value.astype(BF)


def sum_columns(start, width, r, block, grads, weights, keep, send):
    rows = grads.shape[1]
    at = pl.ds(pl.multiple_of(r * block, block), block)
    step = chunk(width, 1536)

    @pl.loop(0, width // step)
    def _(d):
        source = pl.ds(pl.multiple_of(start + d * step, step), step)
        cols = pl.ds(pl.multiple_of(d * step, step), step)
        value = dot_nt(grads[0, at, :], weights[0, source, :])
        value = value + dot_nt(grads[1, at, :], weights[1, source, :])
        store_halves(r, block, rows, cols, value, keep, send)


def back_kernel(n, *refs):
    pieces = refs[:n]
    weights, w_down, near_down, both, keep, send, grads, score, _, held, v_down, sem, sems = refs[n:]
    rows, ff = both.shape[1:]
    block = min(rows, ROWS)
    near = near_down.shape[0]
    step = chunk(near, 1024)
    copy = pltpu.make_async_copy(w_down.at[pl.ds(near, ff - near)], v_down, sem)
    copy.start()
    fetch(pieces, held, sems)

    @pl.loop(0, rows // block)
    def _(r):
        at = pl.ds(pl.multiple_of(r * block, block), block)
        score[at, :] = jnp.zeros((block, 1), F32)

        for f in range(ff // step):
            cols = pl.ds(f * step, step)
            if f * step == near:

                @pl.when(r == 0)
                def _():
                    copy.wait()

            down = near_down[cols, :] if f * step < near else v_down[pl.ds(f * step - near, step), :]
            back = dot_nt(held[at, :], down)
            g, u = both[0, at, cols], both[1, at, cols]
            sig = jax.nn.sigmoid(g)
            silu = g * sig
            score[at, :] += jnp.sum(silu * u * back, axis=1, keepdims=True)
            grads[0, at, cols] = (back * u * sig * (1.0 + g * (1.0 - sig))).astype(BF)
            grads[1, at, cols] = (back * silu).astype(BF)

        sum_columns(0, keep.shape[1], r, block, grads, weights, keep, send)


def rest_kernel(start, weights, grads, score, keep, send):
    rows = grads.shape[1]
    width = keep.shape[1] - LANES
    block, half = min(rows, ROWS), rows // 2

    @pl.loop(0, rows // block)
    def _(r):
        sum_columns(start, width, r, block, grads, weights, keep, send)

    keep[:, pl.ds(width, LANES)] = split3(score[pl.ds(0, half), :]).astype(F32)
    send[:, pl.ds(width, LANES)] = split3(score[pl.ds(half, half), :])


def add_kernel(tail, mine, theirs, *outs):
    width = mine.shape[1] - (LANES if tail else 0)
    at = 0
    for out in outs:
        rows = out.shape[0]
        here = pl.ds(at, rows)
        total = mine[here, pl.ds(0, width)] + theirs[here, pl.ds(0, width)].astype(F32)
        out[:, pl.ds(0, width)] = total.astype(out.dtype)
        if tail:
            last = pl.ds(width, LANES)
            out[:, last] = split3(join3(mine[here, last]) + join3(theirs[here, last])).astype(out.dtype)
        at += rows


def route_kernel(tokens, w_router, routes, relative, weight, sign, pair):
    experts = w_router.shape[0]
    logits = dot_nt(tokens[...], w_router[...])
    label = lax.broadcasted_iota(jnp.int32, logits.shape, 1)
    first, second = label == routes[:, 0:1], label == routes[:, 1:2]
    chosen = [jnp.sum(jnp.where(m, logits, 0.0), axis=1, keepdims=True) for m in (first, second)]
    prob = [jax.nn.sigmoid(chosen[0] - chosen[1]), jax.nn.sigmoid(chosen[1] - chosen[0])]
    pair[...] = jnp.where(first, 1.0, 0.0) - jnp.where(second, 1.0, 0.0)
    first, second = label == relative[:, 0:1], label == relative[:, 1:2]
    weight[:, pl.ds(0, experts)] = jnp.where(first, prob[0], 0.0) + jnp.where(second, prob[1], 0.0)
    weight[:, pl.ds(experts, 1)] = prob[0] * prob[1]
    sign[...] = jnp.where(first, 1.0, 0.0) - jnp.where(second, 1.0, 0.0)


def final_kernel(n, *refs):
    first, second, (weight, sign, pair, router, out, logit_grad) = refs[:n], refs[n : 2 * n], refs[2 * n :]
    lead = first[0].shape[1]
    gap = 0.0
    for s, block in enumerate(second):
        gap = gap + sign[:, s : s + 1] * join3(block[:, pl.ds(out.shape[1] - lead, LANES)])
    grad = weight[:, n : n + 1] * gap
    turned = jnp.broadcast_to(grad, (grad.shape[0], LANES)).T
    logit_grad[0:1, :] = turned[0:1, :]
    logit_grad[1:2, :] = -turned[0:1, :]
    for blocks, cols in ((first, pl.ds(0, lead)), (second, pl.ds(lead, out.shape[1] - lead))):
        total = 0.0
        for s, block in enumerate(blocks):
            total = total + weight[:, s : s + 1] * block[:, pl.ds(0, cols.size)].astype(F32)
        for e in range(n):
            total = total + (grad * pair[:, e : e + 1]) * router[e : e + 1, cols]
        out[:, cols] = total.astype(BF)


def call(kernel, args, outs, specs, scratch=(), limit=None, cost=None, alias={}):
    return pl.pallas_call(
        kernel,
        out_shape=outs,
        in_specs=specs,
        out_specs=[VMEM] * len(outs),
        scratch_shapes=list(scratch),
        compiler_params=pltpu.CompilerParams(vmem_limit_bytes=limit),
        cost_estimate=cost,
        input_output_aliases=alias,
    )(*args)


def shards(hidden, tokens, grad_out, routes, w_router, w_gate, w_up, w_down):
    own, width = tokens.shape
    experts = w_router.shape[1]
    ff = w_gate.shape[2]
    shape = jax.ShapeDtypeStruct
    bits = []
    while (1 << len(bits)) < hidden:
        bits.append(1 << len(bits))
    bits = bits[1:] + bits[:1]

    def along(x, shift):
        return lax.ppermute(x, "expert", [(i, i ^ shift) for i in range(experts)])

    def across(x, bit):
        return lax.ppermute(x, "hidden", [(i, i ^ bit) for i in range(hidden)])

    rows = own * experts * hidden
    macs = rows * width * ff
    lead = width // 2
    rest = width - lead + LANES
    resident_bytes = rows * (2 * width + 8 * LANES) + rows * (ff * 4 + lead * 3 + rest * 3)
    grant = GRANT if rows <= ROWS else resident_bytes + (8 << 20)
    small = min(rows, 2048) * (width + LANES) * 4 + (1 << 20)

    def cost(weights, matmuls):
        return pl.CostEstimate(
            flops=int(2 * matmuls * macs), bytes_accessed=2 * weights * width * ff, transcendentals=0
        )

    def vmem(x):
        return pltpu.with_memory_space_constraint(x, pltpu.VMEM)

    def hbm(x):
        return pltpu.with_memory_space_constraint(x, pltpu.HBM)

    def column(x):
        return jnp.concatenate([x] + [along(x, s) for s in range(1, experts)])

    def spread(pieces, some):
        for bit in some:
            pieces = pieces + [across(piece, bit) for piece in pieces]
        return pieces

    w_gate, w_up, w_down = [hbm(w[0]) for w in (w_gate, w_up, w_down)]
    held = pltpu.VMEM((rows, width), BF)
    pair_of = shape((2, *w_gate.shape), BF)
    def load(k, *args):
        specs = [ANY, VMEM][: len(args)]
        alias = {1: 0} if k else {}
        sem = [pltpu.SemaphoreType.DMA]
        (out,) = call(functools.partial(load_kernel, k), args, [pair_of], specs, sem, grant, cost(0, 0), alias)
        return vmem(out)

    grad_out, weights = lax.optimization_barrier((grad_out, load(0, w_gate)))
    x_column, weights = lax.optimization_barrier((column(tokens), weights))
    x_pieces = spread([x_column], bits[:-1])
    x_pieces[-1], weights = lax.optimization_barrier((x_pieces[-1], load(1, w_up, weights)))
    x_pieces = spread(x_pieces, bits[-1:])
    dy_pieces = spread([column(grad_out)], [bit ^ bits[-1] for bit in bits[:-1]])
    n = len(x_pieces)
    both, weights, near_down = call(
        functools.partial(gate_up_kernel, n),
        x_pieces + [weights, w_down],
        [shape((2, rows, ff), F32), pair_of, shape((ff // 2, width), BF)],
        [ANY] * n + [VMEM, ANY],
        [held, pltpu.SemaphoreType.DMA((n + 1,))],
        grant,
        cost(2, 2),
        {n: 1},
    )
    both, weights, near_down = vmem(both), vmem(weights), vmem(near_down)
    *late, both = lax.optimization_barrier((*dy_pieces[1:], both))
    dy_pieces = spread(dy_pieces[:1] + late, bits[-1:])
    half = len(dy_pieces) // 2
    turned = [bin(i).count("1") % 2 for i in range(half)]
    order = [i + half * turned[i] for i in range(half)] + [i + half - half * turned[i] for i in range(half)]
    dy_pieces = [dy_pieces[i] for i in order]
    keep, send, grads, score, weights = call(
        functools.partial(back_kernel, n),
        dy_pieces + [weights, w_down, near_down, both],
        [shape((rows // 2, lead), F32), shape((rows // 2, lead), BF)]
        + [shape((2, rows, ff), BF), shape((rows, 1), F32), pair_of],
        [ANY] * n + [VMEM, ANY, VMEM, VMEM],
        [
            held,
            pltpu.VMEM((ff - ff // 2, width), BF),
            pltpu.SemaphoreType.DMA,
            pltpu.SemaphoreType.DMA((n,)),
        ],
        grant,
        cost(3, 2),
        {n: 4},
    )
    keep_rest, send_rest = call(
        functools.partial(rest_kernel, lead),
        [vmem(weights), vmem(grads), score],
        [shape((rows // 2, rest), F32), shape((rows // 2, rest), BF)],
        [VMEM] * 3,
        limit=grant,
        cost=cost(1, 1),
    )
    send_rest, routes, w_router, tokens = lax.optimization_barrier((send_rest, routes, w_router, tokens))
    relative = routes ^ lax.axis_index("expert")
    weight, sign, pair = call(
        route_kernel,
        [tokens, w_router.T, routes, relative],
        [shape((own, experts + 1), F32), shape((own, experts), F32), shape((own, experts), F32)],
        [VMEM] * 4,
        limit=small,
    )

    def collect(keep, send, tail):
        add = functools.partial(add_kernel, tail)
        total = keep.shape[1]
        for bit in bits[:0:-1]:
            arrived = across(send, bit)
            outs = [shape((keep.shape[0] // 2, total), kind) for kind in (F32, BF)]
            keep, send = call(add, [keep, arrived], outs, [VMEM] * 2, limit=small)
        arrived = across(send, bits[0])
        outs = [shape((own, total), F32)] + [shape((own, total), BF)] * (experts - 1)
        blocks = call(add, [keep, arrived], outs, [VMEM] * 2, limit=small)
        return [blocks[0]] + [along(blocks[s], s) for s in range(1, experts)]

    first, second = collect(keep, send, False), collect(keep_rest, send_rest, True)
    input_grad, logit_grad = call(
        functools.partial(final_kernel, experts),
        first + second + [weight, sign, pair, w_router.astype(F32).T],
        [shape((own, width), BF), shape((2, own), F32)],
        [VMEM] * (2 * experts + 4),
        limit=small,
    )
    return (input_grad, logit_grad.T)


def solution(mesh):
    row = P(("parts", "expert", "hidden"), None)
    placed = (
        row,
        row,
        row,
        P(),
        P("expert", None, "hidden"),
        P("expert", None, "hidden"),
        P("expert", "hidden", None),
    )
    return jax.shard_map(
        functools.partial(shards, mesh.shape["hidden"]),
        mesh=mesh,
        in_specs=placed,
        out_specs=(row, row),
        check_vma=False,
    )
```

```python
import functools

import jax
import jax.numpy as jnp
from jax import lax
from jax.experimental import pallas as pl
from jax.experimental.pallas import tpu as pltpu
from jax.sharding import PartitionSpec as P

BF = jnp.bfloat16
F32 = jnp.float32
LANES = 128
ROWS = 256
GRANT = 15 << 20
NT = (((1,), (1,)), ((), ()))
ANY = pl.BlockSpec(memory_space=pl.ANY)
VMEM = pl.BlockSpec(memory_space=pltpu.VMEM)


def dot_nt(a, b):
    return lax.dot_general(a, b, NT, preferred_element_type=F32)


def chunk(extent, wanted):
    size = min(extent, wanted)
    while extent % size:
        size -= LANES
    return size


def fetch(pieces, held, sems):
    copies, at = [], 0
    for i, piece in enumerate(pieces):
        rows = piece.shape[0]
        copies.append(pltpu.make_async_copy(piece, held.at[pl.ds(at, rows)], sems.at[i]))
        at += rows
    for copy in copies:
        copy.start()
    for copy in copies:
        copy.wait()


def load_kernel(k, source, *refs):
    half = source.shape[0] // 2
    parts = [pl.ds(i * half, half) for i in range(2)]
    copies = [
        pltpu.make_async_copy(source.at[part], refs[-2].at[k, part], refs[-1].at[i])
        for i, part in enumerate(parts)
    ]
    for copy in copies:
        copy.start()
    for copy in copies:
        copy.wait()


def gate_up_kernel(n, *refs):
    pieces, (weights, w_down, both, _, near_down, held, sems) = refs[:n], refs[n:]
    copy = pltpu.make_async_copy(w_down.at[pl.ds(0, near_down.shape[0])], near_down, sems.at[n])
    copy.start()
    fetch(pieces, held, sems)
    rows, ff = both.shape[1:]
    block, step = min(rows, ROWS), chunk(ff, 1024)

    @pl.loop(0, rows // block)
    def _(r):
        at = pl.ds(pl.multiple_of(r * block, block), block)

        @pl.loop(0, ff // step)
        def _(f):
            cols = pl.ds(pl.multiple_of(f * step, step), step)
            for k in range(2):
                both[k, at, cols] = jnp.dot(held[at, :], weights[k, :, cols], preferred_element_type=F32)

    copy.wait()


def split3(score):
    high = score.astype(BF)
    rest = score - high.astype(F32)
    mid = rest.astype(BF)
    low = (rest - mid.astype(F32)).astype(BF)
    lane = lax.broadcasted_iota(jnp.int32, (score.shape[0], LANES), 1)
    spread = [jnp.broadcast_to(t.astype(F32), lane.shape) for t in (high, mid, low)]
    out = jnp.where(lane == 0, spread[0], jnp.where(lane == 1, spread[1], spread[2]))
    return jnp.where(lane < 3, out, 0.0).astype(BF)


def join3(tail):
    return jnp.sum(tail.astype(F32), axis=1, keepdims=True)


def store_halves(r, block, rows, cols, value, keep, send):
    half = rows // 2
    if rows == block:
        keep[:, cols] = value[:half]
        send[:, cols] = value[half:].astype(BF)
    else:

        @pl.when(r < half // block)
        def _():
            keep[pl.ds(pl.multiple_of(r * block, block), block), cols] = value

        @pl.when(r >= half // block)
        def _():
            send[pl.ds(pl.multiple_of(r * block - half, block), block), cols] = value.astype(BF)


def sum_columns(start, width, r, block, grads, weights, keep, send):
    rows = grads.shape[1]
    at = pl.ds(pl.multiple_of(r * block, block), block)
    step = chunk(width, 1536)

    @pl.loop(0, width // step)
    def _(d):
        source = pl.ds(pl.multiple_of(start + d * step, step), step)
        cols = pl.ds(pl.multiple_of(d * step, step), step)
        value = dot_nt(grads[0, at, :], weights[0, source, :])
        value = value + dot_nt(grads[1, at, :], weights[1, source, :])
        store_halves(r, block, rows, cols, value, keep, send)


def back_kernel(n, *refs):
    pieces = refs[:n]
    weights, w_down, near_down, both, keep, send, grads, score, _, held, v_down, sem, sems = refs[n:]
    rows, ff = both.shape[1:]
    block = min(rows, ROWS)
    near = near_down.shape[0]
    step = chunk(near, 1024)
    copy = pltpu.make_async_copy(w_down.at[pl.ds(near, ff - near)], v_down, sem)
    copy.start()
    fetch(pieces, held, sems)

    @pl.loop(0, rows // block)
    def _(r):
        at = pl.ds(pl.multiple_of(r * block, block), block)
        score[at, :] = jnp.zeros((block, 1), F32)

        for f in range(ff // step):
            cols = pl.ds(f * step, step)
            if f * step == near:

                @pl.when(r == 0)
                def _():
                    copy.wait()

            down = near_down[cols, :] if f * step < near else v_down[pl.ds(f * step - near, step), :]
            back = dot_nt(held[at, :], down)
            g, u = both[0, at, cols], both[1, at, cols]
            sig = jax.nn.sigmoid(g)
            silu = g * sig
            score[at, :] += jnp.sum(silu * u * back, axis=1, keepdims=True)
            grads[0, at, cols] = (back * u * sig * (1.0 + g * (1.0 - sig))).astype(BF)
            grads[1, at, cols] = (back * silu).astype(BF)

        sum_columns(0, keep.shape[1], r, block, grads, weights, keep, send)


def rest_kernel(start, weights, grads, score, keep, send):
    rows = grads.shape[1]
    width = keep.shape[1] - LANES
    block, half = min(rows, ROWS), rows // 2

    @pl.loop(0, rows // block)
    def _(r):
        sum_columns(start, width, r, block, grads, weights, keep, send)

    keep[:, pl.ds(width, LANES)] = split3(score[pl.ds(0, half), :]).astype(F32)
    send[:, pl.ds(width, LANES)] = split3(score[pl.ds(half, half), :])


def add_kernel(tail, mine, theirs, *outs):
    width = mine.shape[1] - (LANES if tail else 0)
    at = 0
    for out in outs:
        rows = out.shape[0]
        here = pl.ds(at, rows)
        total = mine[here, pl.ds(0, width)] + theirs[here, pl.ds(0, width)].astype(F32)
        out[:, pl.ds(0, width)] = total.astype(out.dtype)
        if tail:
            last = pl.ds(width, LANES)
            out[:, last] = split3(join3(mine[here, last]) + join3(theirs[here, last])).astype(out.dtype)
        at += rows


def route_kernel(tokens, w_router, routes, relative, weight, sign, pair):
    experts = w_router.shape[0]
    logits = dot_nt(tokens[...], w_router[...])
    label = lax.broadcasted_iota(jnp.int32, logits.shape, 1)
    first, second = label == routes[:, 0:1], label == routes[:, 1:2]
    chosen = [jnp.sum(jnp.where(m, logits, 0.0), axis=1, keepdims=True) for m in (first, second)]
    prob = [jax.nn.sigmoid(chosen[0] - chosen[1]), jax.nn.sigmoid(chosen[1] - chosen[0])]
    pair[...] = jnp.where(first, 1.0, 0.0) - jnp.where(second, 1.0, 0.0)
    first, second = label == relative[:, 0:1], label == relative[:, 1:2]
    weight[:, pl.ds(0, experts)] = jnp.where(first, prob[0], 0.0) + jnp.where(second, prob[1], 0.0)
    weight[:, pl.ds(experts, 1)] = prob[0] * prob[1]
    sign[...] = jnp.where(first, 1.0, 0.0) - jnp.where(second, 1.0, 0.0)


def final_kernel(n, *refs):
    first, second, (weight, sign, pair, router, out, logit_grad) = refs[:n], refs[n : 2 * n], refs[2 * n :]
    lead = first[0].shape[1]
    gap = 0.0
    for s, block in enumerate(second):
        gap = gap + sign[:, s : s + 1] * join3(block[:, pl.ds(out.shape[1] - lead, LANES)])
    grad = weight[:, n : n + 1] * gap
    turned = jnp.broadcast_to(grad, (grad.shape[0], LANES)).T
    logit_grad[0:1, :] = turned[0:1, :]
    logit_grad[1:2, :] = -turned[0:1, :]
    for blocks, cols in ((first, pl.ds(0, lead)), (second, pl.ds(lead, out.shape[1] - lead))):
        total = 0.0
        for s, block in enumerate(blocks):
            total = total + weight[:, s : s + 1] * block[:, pl.ds(0, cols.size)].astype(F32)
        for e in range(n):
            total = total + (grad * pair[:, e : e + 1]) * router[e : e + 1, cols]
        out[:, cols] = total.astype(BF)


def call(kernel, args, outs, specs, scratch=(), limit=None, cost=None, alias={}):
    return pl.pallas_call(
        kernel,
        out_shape=outs,
        in_specs=specs,
        out_specs=[VMEM] * len(outs),
        scratch_shapes=list(scratch),
        compiler_params=pltpu.CompilerParams(vmem_limit_bytes=limit),
        cost_estimate=cost,
        input_output_aliases=alias,
    )(*args)


def shards(hidden, tokens, grad_out, routes, w_router, w_gate, w_up, w_down):
    own, width = tokens.shape
    experts = w_router.shape[1]
    ff = w_gate.shape[2]
    shape = jax.ShapeDtypeStruct
    bits = []
    while (1 << len(bits)) < hidden:
        bits.append(1 << len(bits))
    bits = bits[1:] + bits[:1]

    def along(x, shift):
        return lax.ppermute(x, "expert", [(i, i ^ shift) for i in range(experts)])

    def across(x, bit):
        return lax.ppermute(x, "hidden", [(i, i ^ bit) for i in range(hidden)])

    rows = own * experts * hidden
    macs = rows * width * ff
    lead = width // 2
    rest = width - lead + LANES
    resident_bytes = rows * (2 * width + 8 * LANES) + rows * (ff * 4 + lead * 3 + rest * 3)
    grant = GRANT if rows <= ROWS else resident_bytes + (8 << 20)
    small = min(rows, 2048) * (width + LANES) * 4 + (1 << 20)

    def cost(weights, matmuls):
        return pl.CostEstimate(
            flops=int(2 * matmuls * macs), bytes_accessed=2 * weights * width * ff, transcendentals=0
        )

    def vmem(x):
        return pltpu.with_memory_space_constraint(x, pltpu.VMEM)

    def hbm(x):
        return pltpu.with_memory_space_constraint(x, pltpu.HBM)

    def column(x):
        return jnp.concatenate([x] + [along(x, s) for s in range(1, experts)])

    def spread(pieces, some):
        for bit in some:
            pieces = pieces + [across(piece, bit) for piece in pieces]
        return pieces

    w_gate, w_up, w_down = [hbm(w[0]) for w in (w_gate, w_up, w_down)]
    held = pltpu.VMEM((rows, width), BF)
    pair_of = shape((2, *w_gate.shape), BF)
    def load(k, *args):
        specs = [ANY, VMEM][: len(args)]
        alias = {1: 0} if k else {}
        sem = [pltpu.SemaphoreType.DMA((2,))]
        (out,) = call(functools.partial(load_kernel, k), args, [pair_of], specs, sem, grant, cost(0, 0), alias)
        return vmem(out)

    grad_out, weights = lax.optimization_barrier((grad_out, load(0, w_gate)))
    x_column, weights = lax.optimization_barrier((column(tokens), weights))
    x_pieces = spread([x_column], bits[:-1])
    x_pieces[-1], weights = lax.optimization_barrier((x_pieces[-1], load(1, w_up, weights)))
    x_pieces = spread(x_pieces, bits[-1:])
    dy_pieces = spread([column(grad_out)], [bit ^ bits[-1] for bit in bits[:-1]])
    n = len(x_pieces)
    both, weights, near_down = call(
        functools.partial(gate_up_kernel, n),
        x_pieces + [weights, w_down],
        [shape((2, rows, ff), F32), pair_of, shape((ff // 2, width), BF)],
        [ANY] * n + [VMEM, ANY],
        [held, pltpu.SemaphoreType.DMA((n + 1,))],
        grant,
        cost(2, 2),
        {n: 1},
    )
    both, weights, near_down = vmem(both), vmem(weights), vmem(near_down)
    *late, both = lax.optimization_barrier((*dy_pieces[1:], both))
    dy_pieces = spread(dy_pieces[:1] + late, bits[-1:])
    half = len(dy_pieces) // 2
    turned = [bin(i).count("1") % 2 for i in range(half)]
    order = [i + half * turned[i] for i in range(half)] + [i + half - half * turned[i] for i in range(half)]
    dy_pieces = [dy_pieces[i] for i in order]
    keep, send, grads, score, weights = call(
        functools.partial(back_kernel, n),
        dy_pieces + [weights, w_down, near_down, both],
        [shape((rows // 2, lead), F32), shape((rows // 2, lead), BF)]
        + [shape((2, rows, ff), BF), shape((rows, 1), F32), pair_of],
        [ANY] * n + [VMEM, ANY, VMEM, VMEM],
        [
            held,
            pltpu.VMEM((ff - ff // 2, width), BF),
            pltpu.SemaphoreType.DMA,
            pltpu.SemaphoreType.DMA((n,)),
        ],
        grant,
        cost(3, 2),
        {n: 4},
    )
    keep_rest, send_rest = call(
        functools.partial(rest_kernel, lead),
        [vmem(weights), vmem(grads), score],
        [shape((rows // 2, rest), F32), shape((rows // 2, rest), BF)],
        [VMEM] * 3,
        limit=grant,
        cost=cost(1, 1),
    )
    send_rest, routes, w_router, tokens = lax.optimization_barrier((send_rest, routes, w_router, tokens))
    relative = routes ^ lax.axis_index("expert")
    weight, sign, pair = call(
        route_kernel,
        [tokens, w_router.T, routes, relative],
        [shape((own, experts + 1), F32), shape((own, experts), F32), shape((own, experts), F32)],
        [VMEM] * 4,
        limit=small,
    )

    def collect(keep, send, tail):
        add = functools.partial(add_kernel, tail)
        total = keep.shape[1]
        for bit in bits[:0:-1]:
            arrived = across(send, bit)
            outs = [shape((keep.shape[0] // 2, total), kind) for kind in (F32, BF)]
            keep, send = call(add, [keep, arrived], outs, [VMEM] * 2, limit=small)
        arrived = across(send, bits[0])
        outs = [shape((own, total), F32)] + [shape((own, total), BF)] * (experts - 1)
        blocks = call(add, [keep, arrived], outs, [VMEM] * 2, limit=small)
        return [blocks[0]] + [along(blocks[s], s) for s in range(1, experts)]

    first, second = collect(keep, send, False), collect(keep_rest, send_rest, True)
    input_grad, logit_grad = call(
        functools.partial(final_kernel, experts),
        first + second + [weight, sign, pair, w_router.astype(F32).T],
        [shape((own, width), BF), shape((2, own), F32)],
        [VMEM] * (2 * experts + 4),
        limit=small,
    )
    return (input_grad, logit_grad.T)


def solution(mesh):
    row = P(("parts", "expert", "hidden"), None)
    placed = (
        row,
        row,
        row,
        P(),
        P("expert", None, "hidden"),
        P("expert", None, "hidden"),
        P("expert", "hidden", None),
    )
    return jax.shard_map(
        functools.partial(shards, mesh.shape["hidden"]),
        mesh=mesh,
        in_specs=placed,
        out_specs=(row, row),
        check_vma=False,
    )
```
